32 devices in a mesh: region: 8 (over z, y), hour: 4 (over x, core).
Axes of the slice: x: 2, y: 2, z: 4, core: 2. Of those that a mesh axis runs over, the one named last changes fastest.
Arguments:
- kkt_inverse: bfloat16 [8, 1024, 1024], P('region'), may hold values from -1 to 2
- demand: float32 [512, 8192], P('hour', 'region'), may hold values from -6 to 6
- cost_quad: float32 [8192], P('region'), may hold values from 0.1 to 2
- cost_lin: float32 [8192], P('region'), may hold values from -1 to 1
- capacity: float32 [8192], P('region'), may hold values from 0.2 to 2
- ramp: float32 [8192], P('region'), may hold values from 0.05 to 1
- gen_start: float32 [8192], P('region'), may hold values from 0 to 1
- boundary_bus: int32 [8, 2, 128], P('region'), may hold values from 0 to 1023
- tie_count: int32 [8], replicated, may hold values from 32 to 128, as said below
- part_bus: int32 [1024, 8], replicated, may hold values from 0 to 8191
- part_share: float32 [1024, 8], replicated, may hold values from 0.05 to 1
- cleared_mw: float32 [4, 128, 1024], P('hour', 'region'), may hold values from -6 to 6
Outputs:
- angles: float32 [512, 8192], P('hour', 'region')
- payment: float32 [4, 128, 1024], P('hour', 'region')
The draws below stay inside these ranges and needn't reach their ends.
Inputs may be any that keep to these rules, and one draw needn't show every extreme that they name: Tie lines pair up in order: slots below tie_count[r] of region r's right block meet the same slots of the next region's left block (the last region's next is region 0); some region has 128 live tie lines.
All inputs are finite; a program needn't handle non-finite values.
Results may differ from the reference program's by a relative error of at most 0.0062.
Values may be sent and summed in bfloat16 or wider, within the bound.
No kernel may reach another device: no remote copies, remote signals or barrier semaphores. Data moves between devices by JAX's collectives and lax.ppermute only.
A program may use at most 64 MiB of HBM per device.

```python
import math
import jax
import jax.numpy as jnp
import numpy as np
from jax import lax

B = 1024
NS = 128
PARTS_SIZE = 1024
TAPS = 8
ITERS = 2
H_DEV = 128
REGIONS = 8
BUSES = 8192
HOURS = 512


def draw_kkt_inverse(key, part):
    diag_key = jax.random.fold_in(key, 11)
    off_key = jax.random.fold_in(key, 12)
    row_ids = jnp.arange(B)[:, None]
    col_ids = jnp.arange(B)[None, :]
    diagonal = jax.random.uniform(diag_key, (REGIONS, B, 1), jnp.float32, 0.6, 1.4)
    spread = jax.random.normal(off_key, (REGIONS, B, B), jnp.float32) * (0.6 * B ** (-0.5))
    return jnp.where(row_ids == col_ids, diagonal, spread).astype(jnp.bfloat16)


def draw_tie_count(key, part):
    counts = jax.random.randint(jax.random.fold_in(key, 21), (REGIONS,), NS // 4, NS + 1)
    position = jax.random.randint(jax.random.fold_in(key, 22), (), 0, REGIONS)
    return counts.at[position].set(NS).astype(jnp.int32)


def set_ends(values, key, least, top_value):
    longest = values.shape.index(max(values.shape))
    spots = []
    for shift in (0, 1):
        where = [jax.random.randint(jax.random.fold_in(key, axis), (), 0, length) for axis, length in enumerate(values.shape)]
        where[longest] = (where[longest] + shift) % values.shape[longest]
        spots.append(tuple(where))
    return values.at[spots[0]].set(least).at[spots[1]].set(top_value)


def block_scale(rng, dims, cuts, least, high):
    factor_of, own = 1.0, jax.random.fold_in(rng, 6)
    for dim, parts in cuts:
        heights = jnp.exp(jax.random.uniform(jax.random.fold_in(own, dim), (parts,), jnp.float32, least / len(cuts), high / len(cuts)))
        factor_of = factor_of * jnp.repeat(heights, dims[dim] // parts).reshape([-1 if axis == dim else 1 for axis in range(len(dims))])
    return factor_of


def rank_bounds(amount, lean):
    weights = [(1 << 20) // math.isqrt(standing ** lean) + 1 for standing in range(1, amount + 1)]
    scale = 1 + sum(weights) // (1 << 30)
    return np.cumsum(np.array([max(1, weight // scale) for weight in weights]))


def ranked(stream_key, dims, number_of, slope):
    grid = rank_bounds(number_of, slope)
    pick = jax.random.randint(jax.random.fold_in(stream_key, 1), dims, 0, int(grid[number_of - 1]))
    grade = jnp.searchsorted(jnp.asarray(grid, jnp.int32), pick, side="right")
    return jax.random.permutation(jax.random.fold_in(stream_key, 2), number_of)[grade].astype(jnp.int32)


def noise(rng, extent, scale, bound, cuts=(), kind=jnp.bfloat16):
    values = scale * jax.random.normal(rng, extent, jnp.float32)
    if cuts:
        values = values * block_scale(rng, extent, cuts, -0.22, 0.18)
    return jnp.clip(values, -bound, bound).astype(kind)


def setup_inputs(seed: int = 0) -> dict:
    streams_of = jax.random.split(jax.random.key(seed), 13)
    kkt_inverse = draw_kkt_inverse(jax.random.fold_in(streams_of[12], 71), 0)
    demand = noise(streams_of[1], (HOURS, BUSES), 1.0, 6.0, ((0, 4), (1, 8)), jnp.float32)
    cost_quad = jnp.clip(jnp.exp(math.log(2.0) - 2.9957323 * jax.random.uniform(streams_of[2], (BUSES,), jnp.float32) ** block_scale(streams_of[2], (BUSES,), ((0, 8),), -0.2, 0.2)), 0.1, 2.0)
    cost_lin = jnp.clip(jax.random.uniform(streams_of[3], (BUSES,), jnp.float32, -1.0, 1.0) * block_scale(streams_of[3], (BUSES,), ((0, 8),), -0.4, 0.0), -1.0, 1.0)
    capacity = jnp.clip(jnp.exp(math.log(2.0) - 2.3025851 * jax.random.uniform(streams_of[4], (BUSES,), jnp.float32) ** block_scale(streams_of[4], (BUSES,), ((0, 8),), -0.2, 0.2)), 0.2, 2.0)
    ramp = jnp.clip(jnp.exp(math.log(1.0) - 2.9957323 * jax.random.uniform(streams_of[5], (BUSES,), jnp.float32) ** block_scale(streams_of[5], (BUSES,), ((0, 8),), -0.2, 0.2)), 0.05, 1.0)
    gen_start = jnp.clip(1.0 * jax.random.uniform(streams_of[6], (BUSES,), jnp.float32) ** block_scale(streams_of[6], (BUSES,), ((0, 8),), -0.2, 0.2), 0.0, 1.0)
    boundary_bus = set_ends(jax.random.randint(streams_of[7], (REGIONS, 2, NS), 0, B), jax.random.fold_in(streams_of[7], 1), 0, B - 1).astype(jnp.int32)
    tie_count = draw_tie_count(jax.random.fold_in(streams_of[12], 71), 0)
    part_bus = set_ends(ranked(streams_of[9], (PARTS_SIZE, TAPS), BUSES, 2), jax.random.fold_in(streams_of[9], 3), 0, BUSES - 1).astype(jnp.int32)
    part_share = jnp.clip(jnp.exp(jax.random.uniform(streams_of[10], (PARTS_SIZE, TAPS), jnp.float32, math.log(0.05), math.log(1.0))), 0.05, 1.0)
    cleared_mw = noise(streams_of[11], (HOURS // H_DEV, H_DEV, PARTS_SIZE), 1.0, 6.0, ((0, 4), (1, 8)), jnp.float32)
    return dict(kkt_inverse=kkt_inverse, demand=demand, cost_quad=cost_quad, cost_lin=cost_lin, capacity=capacity, ramp=ramp, gen_start=gen_start, boundary_bus=boundary_bus, tie_count=tie_count, part_bus=part_bus, part_share=part_share, cleared_mw=cleared_mw)


def solve_regions(kkt_inverse, right_side):
    hour_count = right_side.shape[0]
    blocks = right_side.reshape(hour_count, REGIONS, B).transpose(1, 0, 2)

    def solve_block(operands):
        matrix, rhs_block = operands
        return jnp.dot(rhs_block.astype(jnp.float32), matrix.astype(jnp.float32).T, preferred_element_type=jnp.float32)

    solved = lax.map(solve_block, (kkt_inverse, blocks))
    return solved.transpose(1, 0, 2).reshape(hour_count, REGIONS * B)


def reference(kkt_inverse, demand, cost_quad, cost_lin, capacity, ramp, gen_start, boundary_bus, tie_count, part_bus, part_share, cleared_mw):
    hour_count = demand.shape[0]
    offsets = (jnp.arange(REGIONS, dtype=jnp.int32) * B)[:, None, None]
    columns = (boundary_bus + offsets).reshape(-1).astype(jnp.int32)
    slot_ids = jnp.arange(NS, dtype=jnp.int32)
    left_live = slot_ids[None, :] < jnp.roll(tie_count, 1)[:, None]
    right_live = slot_ids[None, :] < tie_count[:, None]
    live_mask = jnp.stack([left_live, right_live], axis=1).astype(jnp.float32).reshape(-1)
    generation = jnp.zeros((hour_count, BUSES), jnp.float32)
    dual_var = jnp.zeros((hour_count, BUSES), jnp.float32)
    tie_mean = jnp.zeros((hour_count, REGIONS * 2 * NS), jnp.float32)
    tie_dual = jnp.zeros((hour_count, REGIONS * 2 * NS), jnp.float32)
    angles = generation
    for iteration in range(ITERS):
        tie_term = jnp.zeros((hour_count, BUSES), jnp.float32).at[:, columns].add(live_mask * (tie_mean - tie_dual))
        right_side = (demand + (generation - dual_var) + tie_term).astype(jnp.bfloat16)
        right_side = lax.optimization_barrier(right_side)
        angles = solve_regions(kkt_inverse, right_side)
        at_ends = angles[:, columns]
        tie_ends = at_ends + tie_dual
        shaped = tie_ends.reshape(hour_count, REGIONS, 2, NS)
        far_ends = jnp.stack([jnp.roll(shaped[:, :, 1], 1, axis=1), jnp.roll(shaped[:, :, 0], -1, axis=1)], axis=2).reshape(hour_count, -1)
        tie_mean = live_mask * (tie_ends + far_ends) * 0.5
        tie_dual = live_mask * (tie_dual + at_ends - tie_mean)
        prior_gen = jnp.concatenate([gen_start[None, :], generation[:-1]], axis=0)
        target = (angles + dual_var - cost_lin) / (cost_quad + 1.0)
        limited = jnp.minimum(jnp.maximum(target, prior_gen - ramp), prior_gen + ramp)
        generation = jnp.minimum(jnp.maximum(limited, 0.0), capacity)
        dual_var = dual_var + angles - generation
    prices_bf = dual_var.astype(jnp.bfloat16)
    picked = prices_bf[:, part_bus].astype(jnp.float32)
    prices = jnp.sum(picked * part_share, axis=-1)
    payment = cleared_mw * prices.reshape(cleared_mw.shape)
    return angles, payment
```

```python
import functools

import jax
import jax.numpy as jnp
from jax import lax
from jax.experimental import pallas as pl
from jax.experimental.pallas import tpu as pltpu
from jax.sharding import PartitionSpec as P

BF16 = jnp.bfloat16
F32 = jnp.float32
VMEM = pl.BlockSpec(memory_space=pltpu.VMEM)
SMEM = pl.BlockSpec(memory_space=pltpu.SMEM)
NT = (((1,), (1,)), ((), ()))
CHUNKS = 4


def shifted(shard, axis, by):
    length = lax.axis_size(axis)
    return lax.ppermute(shard, axis, [(i, (i + by) % length) for i in range(length)])


def from_behind(value, axis):
    count = lax.axis_size(axis)
    return lax.ppermute(value, axis, [(source, source + 1) for source in range(count - 1)])


def slot_rows(bus_ref, side, buses):
    slots = bus_ref.shape[1]
    ids = lax.broadcasted_iota(jnp.int32, (buses, slots), 0)
    return (ids == bus_ref[pl.ds(side, 1), :]).astype(F32).astype(BF16)


def first_kernel(
    demand_ref, matrix_ref, bus_ref, quad_ref, lin_ref, cap_ref, ramp_ref, start_ref,
    angles_ref, left_ref, right_ref, edge_ref, matrix_vmem, sems,
):
    buses = matrix_ref.shape[0]
    depth = buses // CHUNKS
    copies = []
    for c in range(CHUNKS):
        rows = pl.ds(c * depth, depth)
        copies.append(pltpu.make_async_copy(matrix_ref.at[rows], matrix_vmem.at[rows], sems.at[c]))
        copies[-1].start()
    right_side = demand_ref[...].astype(BF16)
    one_left = slot_rows(bus_ref, 0, buses)
    one_right = slot_rows(bus_ref, 1, buses)
    left = right = None
    for c in range(CHUNKS):
        rows = pl.ds(c * depth, depth)
        copies[c].wait()
        part = lax.dot_general(right_side, matrix_vmem[rows, :], NT, preferred_element_type=F32)
        angles_ref[:, rows] = part
        part = part.astype(BF16)
        lo, hi = c * depth, (c + 1) * depth
        left_part = jnp.dot(part, one_left[lo:hi], preferred_element_type=F32)
        right_part = jnp.dot(part, one_right[lo:hi], preferred_element_type=F32)
        left = left_part if left is None else left + left_part
        right = right_part if right is None else right + right_part
    left_ref[...] = left.astype(BF16)
    right_ref[...] = right.astype(BF16)
    hours = angles_ref.shape[0]
    tail = angles_ref[pl.ds(hours - 8, 8), :]
    target = (tail - lin_ref[...]) / (quad_ref[...] + 1.0)
    limited = jnp.minimum(jnp.maximum(target, -ramp_ref[...]), ramp_ref[...])
    edge_ref[...] = jnp.minimum(jnp.maximum(limited, 0.0), cap_ref[...])


def middle_kernel(
    angles_ref, demand_ref, matrix_ref, bus_ref, quad_ref, lin_ref, cap_ref, ramp_ref, start_ref,
    part_bus_ref, part_share_ref,
    base_ref, slot_matrix_ref, dual_ref, low_ref, high_ref, weight_ref,
    gen_scratch,
):
    hours, buses = angles_ref.shape
    region = lax.axis_index("region")
    block = lax.axis_index("hour")
    cap = cap_ref[...]
    ramp = ramp_ref[...]
    angles = angles_ref[...]
    row = lax.broadcasted_iota(jnp.int32, (hours, buses), 0)
    first = jnp.logical_and(row == 0, block == 0)
    prior = jnp.where(first, jnp.broadcast_to(start_ref[...], (hours, buses)), 0.0)
    target = (angles - lin_ref[...]) / (quad_ref[...] + 1.0)
    limited = jnp.minimum(jnp.maximum(target, prior - ramp), prior + ramp)
    generation = jnp.minimum(jnp.maximum(limited, 0.0), cap)
    dual = angles - generation
    dual_ref[...] = dual
    right_side = (demand_ref[...] + (generation - dual)).astype(BF16)
    before = pltpu.roll(generation, 1, 0)
    low_ref[...] = jnp.minimum(jnp.maximum(before - ramp, 0.0), cap)
    high_ref[...] = jnp.minimum(jnp.maximum(before + ramp, 0.0), cap)
    matrix = matrix_ref[...]
    base_ref[...] = lax.dot_general(right_side, matrix, NT, preferred_element_type=F32)
    slots = bus_ref.shape[1]
    for side in range(2):
        one = slot_rows(bus_ref, side, buses)
        picked = lax.dot_general(one, matrix, (((0,), (1,)), ((), ())), preferred_element_type=F32)
        slot_matrix_ref[pl.ds(side * slots, slots), :] = picked.astype(BF16)
    taps = part_bus_ref.shape[1]
    local = jnp.transpose(part_bus_ref[...]) - region * buses
    share = jnp.transpose(part_share_ref[...])
    parts = local.shape[1]
    step = 16
    ids = lax.broadcasted_iota(jnp.int32, (step, parts), 0)

    def body(i, carry):
        here = ids + i * step
        total = jnp.zeros((step, parts), F32)
        for k in range(taps):
            total = total + jnp.where(here == local[k : k + 1], share[k : k + 1], 0.0)
        weight_ref[pl.ds(pl.multiple_of(i * step, step), step), :] = total.astype(BF16)
        return carry

    lax.fori_loop(0, buses // step, body, 0)


def last_kernel(
    base_ref, slot_matrix_ref, from_left_ref, from_right_ref, edge_ref, dual_ref, low_ref, high_ref,
    weight_ref, quad_ref, lin_ref, cap_ref, ramp_ref, start_ref, count_ref,
    angles_ref, price_ref,
):
    hours, buses = base_ref.shape
    slots = from_left_ref.shape[1]
    region = lax.axis_index("region")
    region_count = count_ref.shape[0]
    block = lax.axis_index("hour")
    left_count = count_ref[lax.rem(region + region_count - 1, region_count)]
    right_count = count_ref[region]
    ids = lax.broadcasted_iota(jnp.int32, (hours, slots), 1)
    zero = jnp.zeros((hours, slots), F32)
    left = jnp.where(ids < left_count, from_left_ref[...].astype(F32), zero).astype(BF16)
    right = jnp.where(ids < right_count, from_right_ref[...].astype(F32), zero).astype(BF16)
    angles = base_ref[...]
    angles = angles + jnp.dot(left, slot_matrix_ref[pl.ds(0, slots), :], preferred_element_type=F32)
    angles = angles + jnp.dot(right, slot_matrix_ref[pl.ds(slots, slots), :], preferred_element_type=F32)
    angles_ref[...] = angles
    cap = cap_ref[...]
    ramp = ramp_ref[...]
    prior = jnp.where(block == 0, start_ref[...], edge_ref[pl.ds(7, 1), :])
    low_first = jnp.minimum(jnp.maximum(prior - ramp, 0.0), cap)
    high_first = jnp.minimum(jnp.maximum(prior + ramp, 0.0), cap)
    first = lax.broadcasted_iota(jnp.int32, (hours, buses), 0) == 0
    low = jnp.where(first, low_first, low_ref[...])
    high = jnp.where(first, high_first, high_ref[...])
    total = angles + dual_ref[...]
    target = (total - lin_ref[...]) / (quad_ref[...] + 1.0)
    generation = jnp.minimum(jnp.maximum(target, low), high)
    lmp = (total - generation).astype(BF16)
    price_ref[...] = jnp.dot(lmp, weight_ref[...], preferred_element_type=F32).astype(BF16)


def pay_kernel(pieces_ref, cleared_ref, out_ref):
    total = pieces_ref[0].astype(F32)
    for i in range(1, pieces_ref.shape[0]):
        total = total + pieces_ref[i].astype(F32)
    out_ref[...] = cleared_ref[...] * total


def shards(
    kkt_inverse, demand, cost_quad, cost_lin, capacity, ramp, gen_start, boundary_bus, tie_count,
    part_bus, part_share, cleared_mw,
):
    region_count = lax.axis_size("region")
    hours, buses = demand.shape
    matrix = kkt_inverse[0]
    bus = boundary_bus[0]
    slots = bus.shape[1]
    parts = part_bus.shape[0]
    quad, lin, cap, ramp, start = (
        v.reshape(1, buses) for v in (cost_quad, cost_lin, capacity, ramp, gen_start)
    )
    wide = jax.ShapeDtypeStruct((hours, buses), F32)
    ends = jax.ShapeDtypeStruct((hours, slots), BF16)
    params = pltpu.CompilerParams(vmem_limit_bytes=32 * 1024 * 1024)
    angles, left, right, edge = pl.pallas_call(
        first_kernel,
        out_shape=(wide, ends, ends, jax.ShapeDtypeStruct((8, buses), F32)),
        in_specs=[VMEM, pl.BlockSpec(memory_space=pl.ANY)] + [VMEM] * 6,
        out_specs=(VMEM,) * 4,
        scratch_shapes=[pltpu.VMEM((buses, buses), BF16), pltpu.SemaphoreType.DMA((CHUNKS,))],
        compiler_params=params,
        name="first_angles",
    )(demand, matrix, bus, quad, lin, cap, ramp, start)
    from_left = shifted(right, "region", 1)
    from_right = shifted(left, "region", -1)
    edge = from_behind(edge, "hour")
    base, slot_matrix, dual, low, high, weight = pl.pallas_call(
        middle_kernel,
        out_shape=(
            wide,
            jax.ShapeDtypeStruct((2 * slots, buses), BF16),
            wide,
            wide,
            wide,
            jax.ShapeDtypeStruct((buses, parts), BF16),
        ),
        in_specs=[VMEM] * 11,
        out_specs=(VMEM,) * 6,
        scratch_shapes=[pltpu.VMEM((hours, buses), F32)],
        compiler_params=params,
        cost_estimate=pl.CostEstimate(flops=2 * 384 * buses * buses, bytes_accessed=12 << 20, transcendentals=0),
        name="middle",
    )(angles, demand, matrix, bus, quad, lin, cap, ramp, start, part_bus, part_share)
    angles, price = pl.pallas_call(
        last_kernel,
        out_shape=(wide, jax.ShapeDtypeStruct((hours, parts), BF16)),
        in_specs=[VMEM] * 14 + [SMEM],
        out_specs=(VMEM, VMEM),
        compiler_params=params,
        name="second_angles",
    )(base, slot_matrix, from_left, from_right, edge, dual, low, high, weight, quad, lin, cap, ramp, start, tie_count)
    pieces = price.reshape(region_count, hours // region_count, parts)
    pieces = lax.all_to_all(pieces, "region", 0, 0, tiled=True)
    payment = pl.pallas_call(
        pay_kernel,
        out_shape=jax.ShapeDtypeStruct(cleared_mw.shape[1:], F32),
        in_specs=[VMEM, VMEM],
        out_specs=VMEM,
        compiler_params=params,
        name="payment",
    )(pieces, cleared_mw[0])
    return angles, payment[None]


def solution(mesh):
    return jax.shard_map(
        shards,
        mesh=mesh,
        in_specs=(
            P("region", None, None),
            P("hour", "region"),
            P("region"),
            P("region"),
            P("region"),
            P("region"),
            P("region"),
            P("region", None, None),
            P(),
            P(),
            P(),
            P("hour", "region", None),
        ),
        out_specs=(P("hour", "region"), P("hour", "region", None)),
        check_vma=False,
    )
```

```python
import jax
import jax.numpy as jnp
from jax import lax
from jax.experimental import pallas as pl
from jax.experimental.pallas import tpu as pltpu
from jax.sharding import PartitionSpec as P

BF16 = jnp.bfloat16
F32 = jnp.float32
I32 = jnp.int32
VMEM = pl.BlockSpec(memory_space=pltpu.VMEM)
HBM = pl.BlockSpec(memory_space=pltpu.HBM)
NT = (((1,), (1,)), ((), ()))
CHUNKS = 4
LANES = 128
PARAMS = pltpu.CompilerParams(vmem_limit_bytes=16 * 1024 * 1024)


def swapped(value, axis, parity):
    count = lax.axis_size(axis)
    pairs = []
    for low in range(parity, count, 2):
        high = (low + 1) % count
        pairs += [(low, high), (high, low)]
    return lax.ppermute(value, axis, pairs)


def from_behind(value, axis):
    count = lax.axis_size(axis)
    return lax.ppermute(value, axis, [(i, (i + 1) % count) for i in range(count)])


def first_kernel(
    demand_in, matrix_in, bus_in, quad_in, lin_in, cap_in, ramp_in, start_in, count_in, part_in, share_in,
    angles_ref, inner_ref, outer_ref, edge_ref, matrix_ref, demand_ref, params_ref, slot_ref, part_ref, share_ref,
    bus_ref, quad_ref, lin_ref, cap_ref, ramp_ref, start_ref, count_ref, sems,
):
    buses = matrix_ref.shape[0]
    depth = buses // CHUNKS
    small = [
        (bus_in, bus_ref), (count_in, count_ref), (quad_in, quad_ref), (lin_in, lin_ref), (cap_in, cap_ref),
        (ramp_in, ramp_ref), (start_in, start_ref), (part_in, part_ref), (share_in, share_ref),
    ]
    demand_copy = pltpu.make_async_copy(demand_in, demand_ref, sems.at[0])
    demand_copy.start()
    copies = []
    for c in range(CHUNKS):
        rows = pl.ds(c * depth, depth)
        copies.append(pltpu.make_async_copy(matrix_in.at[rows], matrix_ref.at[rows], sems.at[1 + c]))
        copies[-1].start()
    small_copies = [
        pltpu.make_async_copy(source, target, sems.at[1 + CHUNKS + i]) for i, (source, target) in enumerate(small)
    ]
    for copy in small_copies:
        copy.start()
    for copy in small_copies:
        copy.wait()

    region = lax.axis_index("region")
    region_count = count_ref.shape[1]
    odd = lax.rem(region, 2)
    slots = bus_ref.shape[1]
    left_region = lax.rem(region + region_count - 1, region_count)
    regions = lax.broadcasted_iota(I32, count_ref.shape, 1)
    counts = count_ref[...]
    left_count = jnp.sum(jnp.where(regions == left_region, counts, 0), axis=1, keepdims=True)
    right_count = jnp.sum(jnp.where(regions == region, counts, 0), axis=1, keepdims=True)
    ids = lax.broadcasted_iota(I32, (1, slots), 1)
    left_bus = jnp.where(ids < left_count, bus_ref[0:1, :], -1)
    right_bus = jnp.where(ids < right_count, bus_ref[1:2, :], -1)
    inner_bus = jnp.where(odd == 0, right_bus, left_bus)
    outer_bus = jnp.where(odd == 0, left_bus, right_bus)
    slot_ref[...] = jnp.full(slot_ref.shape, -1, I32)
    slot_ref[0:1, :] = inner_bus
    slot_ref[1:2, :] = outer_bus
    params_ref[...] = jnp.zeros(params_ref.shape, F32)
    inverse = 1.0 / (quad_ref[...] + 1.0)
    params_ref[0:1, :] = inverse
    params_ref[1:2, :] = lin_ref[...]
    params_ref[2:3, :] = cap_ref[...]
    params_ref[3:4, :] = ramp_ref[...]
    params_ref[4:5, :] = start_ref[...]

    demand_copy.wait()
    right_side = demand_ref[...].astype(BF16)
    both_bus = jnp.concatenate([inner_bus, outer_bus], axis=1)
    ends = None
    for c in range(CHUNKS):
        rows = pl.ds(c * depth, depth)
        row_ids = lax.broadcasted_iota(I32, (depth, 2 * slots), 0) + c * depth
        one = (row_ids == both_bus).astype(F32).astype(BF16)
        copies[c].wait()
        part = lax.dot_general(right_side, matrix_ref[rows, :], NT, preferred_element_type=F32)
        angles_ref[:, rows] = part
        picked = jnp.dot(part.astype(BF16), one, preferred_element_type=F32)
        ends = picked if ends is None else ends + picked
    ends = ends.astype(BF16)
    inner_ref[...] = ends[:, :slots]
    outer_ref[...] = ends[:, slots:]
    hours = angles_ref.shape[0]
    tail = angles_ref[pl.ds(hours - 8, 8), :][7:8, :]
    target = (tail - lin_ref[...]) * inverse
    limited = jnp.minimum(jnp.maximum(target, -ramp_ref[...]), ramp_ref[...])
    edge_ref[...] = jnp.minimum(jnp.maximum(limited, 0.0), cap_ref[...])


def middle_kernel(
    angles_ref, demand_ref, matrix_ref, params_ref, slot_ref, part_ref, share_ref,
    base_ref, slot_matrix_ref, dual_ref, low_ref, high_ref, weight_ref,
):
    hours, buses = angles_ref.shape
    region = lax.axis_index("region")
    block = lax.axis_index("hour")
    inverse, lin, cap, ramp, start = (params_ref[i : i + 1, :] for i in range(5))
    angles = angles_ref[...]
    row = lax.broadcasted_iota(I32, (hours, buses), 0)
    first = jnp.logical_and(row == 0, block == 0)
    prior = jnp.where(first, jnp.broadcast_to(start, (hours, buses)), 0.0)
    target = (angles - lin) * inverse
    limited = jnp.minimum(jnp.maximum(target, prior - ramp), prior + ramp)
    generation = jnp.minimum(jnp.maximum(limited, 0.0), cap)
    dual = angles - generation
    dual_ref[...] = dual
    right_side = (demand_ref[...] + (generation - dual)).astype(BF16)
    before = pltpu.roll(generation, 1, 0)
    low_ref[...] = jnp.minimum(jnp.maximum(before - ramp, 0.0), cap)
    high_ref[...] = jnp.minimum(jnp.maximum(before + ramp, 0.0), cap)
    slots = slot_ref.shape[1]
    columns = jnp.transpose(slot_ref[...])
    lane = lax.broadcasted_iota(I32, (slots, buses), 1)
    picks = [(lane == columns[:, side : side + 1]).astype(F32).astype(BF16) for side in range(2)]
    stacked = jnp.concatenate([right_side] + picks, axis=0)
    product = lax.dot_general(stacked, matrix_ref[...], NT, preferred_element_type=F32)
    base_ref[...] = product[:hours]
    slot_matrix_ref[...] = product[hours:].astype(BF16)

    taps, parts = part_ref.shape
    local = part_ref[...] - region * buses
    inside = jnp.logical_and(local >= 0, local < buses)
    local = jnp.where(inside, local, -1)
    upper = lax.shift_right_arithmetic(local, 7)
    lower = jnp.where(inside, jnp.bitwise_and(local, LANES - 1), -1)
    share = share_ref[...]
    half = LANES // 2
    for group in range(parts // LANES):
        lanes = slice(group * LANES, (group + 1) * LANES)
        for part in range(2):
            ids = lax.broadcasted_iota(I32, (half, LANES), 0) + part * half
            values = [
                jnp.where(ids == lower[k : k + 1, lanes], share[k : k + 1, lanes], 0.0).astype(BF16) for k in range(taps)
            ]
            for a in range(buses // LANES):
                total = None
                for k in range(taps):
                    mask = jnp.where(upper[k : k + 1, lanes] == a, 1.0, 0.0)
                    mask = jnp.broadcast_to(mask, (half, LANES)).astype(BF16)
                    term = values[k] * mask
                    total = term if total is None else total + term
                weight_ref[a * LANES + part * half : a * LANES + (part + 1) * half, lanes] = total


def last_kernel(
    base_ref, slot_matrix_ref, inner_ref, outer_ref, edge_ref, dual_ref, low_ref, high_ref, weight_ref, params_ref,
    angles_out, price_ref,
    angles_ref, sem,
):
    hours, buses = base_ref.shape
    slots = inner_ref.shape[1]
    block = lax.axis_index("hour")
    inverse, lin, cap, ramp, start = (params_ref[i : i + 1, :] for i in range(5))
    far = jnp.concatenate([inner_ref[...], outer_ref[...]], axis=1)
    angles = base_ref[...] + jnp.dot(far, slot_matrix_ref[...], preferred_element_type=F32)
    angles_ref[...] = angles
    copy = pltpu.make_async_copy(angles_ref, angles_out, sem)
    copy.start()
    prior = jnp.where(block == 0, start, edge_ref[...])
    low_first = jnp.minimum(jnp.maximum(prior - ramp, 0.0), cap)
    high_first = jnp.minimum(jnp.maximum(prior + ramp, 0.0), cap)
    first = lax.broadcasted_iota(I32, (hours, buses), 0) == 0
    low = jnp.where(first, low_first, low_ref[...])
    high = jnp.where(first, high_first, high_ref[...])
    total = angles + dual_ref[...]
    target = (total - lin) * inverse
    generation = jnp.minimum(jnp.maximum(target, low), high)
    lmp = (total - generation).astype(BF16)
    price_ref[...] = jnp.dot(lmp, weight_ref[...], preferred_element_type=F32).astype(BF16)
    copy.wait()


def pay_kernel(pieces_ref, cleared_ref, out_ref):
    total = pieces_ref[0].astype(F32)
    for i in range(1, pieces_ref.shape[0]):
        total = total + pieces_ref[i].astype(F32)
    out_ref[...] = cleared_ref[...] * total


def shards(
    kkt_inverse, demand, cost_quad, cost_lin, capacity, ramp, gen_start, boundary_bus, tie_count,
    part_bus, part_share, cleared_mw,
):
    region_count = lax.axis_size("region")
    hours, buses = demand.shape
    slots = boundary_bus.shape[2]
    parts, taps = part_bus.shape
    rows = [v.reshape(1, buses) for v in (cost_quad, cost_lin, capacity, ramp, gen_start)]
    wide = jax.ShapeDtypeStruct((hours, buses), F32)
    row = jax.ShapeDtypeStruct((1, buses), F32)
    square = jax.ShapeDtypeStruct((buses, buses), BF16)
    ends = jax.ShapeDtypeStruct((hours, slots), BF16)
    angles, inner, outer, edge, matrix, demand, params, slot_bus, part_bus, part_share = pl.pallas_call(
        first_kernel,
        out_shape=(
            wide, ends, ends, row, square, wide,
            jax.ShapeDtypeStruct((8, buses), F32),
            jax.ShapeDtypeStruct((8, slots), I32),
            jax.ShapeDtypeStruct((taps, parts), I32),
            jax.ShapeDtypeStruct((taps, parts), F32),
        ),
        in_specs=[HBM] * 11,
        out_specs=(VMEM,) * 10,
        scratch_shapes=[pltpu.VMEM((2, slots), I32)]
        + [pltpu.VMEM((1, buses), F32)] * 5
        + [pltpu.VMEM((1, region_count), I32), pltpu.SemaphoreType.DMA((CHUNKS + 10,))],
        compiler_params=PARAMS,
        name="first_angles",
    )(
        *(
            pltpu.with_memory_space_constraint(v, pltpu.HBM)
            for v in (
                demand, kkt_inverse[0], boundary_bus[0], *rows, tie_count.reshape(1, region_count),
                part_bus.T, part_share.T,
            )
        )
    )
    outer = swapped(outer, "region", 1)
    inner = swapped(inner, "region", 0)
    edge = from_behind(edge, "hour")
    base, slot_matrix, dual, low, high, weight = pl.pallas_call(
        middle_kernel,
        out_shape=(
            wide,
            jax.ShapeDtypeStruct((2 * slots, buses), BF16),
            wide,
            wide,
            wide,
            jax.ShapeDtypeStruct((buses, parts), BF16),
        ),
        in_specs=[VMEM] * 7,
        out_specs=(VMEM,) * 6,
        compiler_params=PARAMS,
        cost_estimate=pl.CostEstimate(flops=2 * 384 * buses * buses, bytes_accessed=12 << 20, transcendentals=0),
        name="middle",
    )(angles, demand, matrix, params, slot_bus, part_bus, part_share)
    angles, price = pl.pallas_call(
        last_kernel,
        out_shape=(wide, jax.ShapeDtypeStruct((hours, parts), BF16)),
        in_specs=[VMEM] * 10,
        out_specs=(HBM, VMEM),
        scratch_shapes=[pltpu.VMEM((hours, buses), F32), pltpu.SemaphoreType.DMA],
        compiler_params=PARAMS,
        name="second_angles",
    )(base, slot_matrix, inner, outer, edge, dual, low, high, weight, params)
    pieces = price.reshape(region_count, hours // region_count, parts)
    pieces = lax.all_to_all(pieces, "region", 0, 0, tiled=True)
    payment = pl.pallas_call(
        pay_kernel,
        out_shape=jax.ShapeDtypeStruct(cleared_mw.shape[1:], F32),
        in_specs=[VMEM, VMEM],
        out_specs=VMEM,
        compiler_params=PARAMS,
        name="payment",
    )(pieces, cleared_mw[0])
    return angles, payment[None]


def solution(mesh):
    return jax.shard_map(
        shards,
        mesh=mesh,
        in_specs=(
            P("region", None, None),
            P("hour", "region"),
            P("region"),
            P("region"),
            P("region"),
            P("region"),
            P("region"),
            P("region", None, None),
            P(),
            P(),
            P(),
            P("hour", "region", None),
        ),
        out_specs=(P("hour", "region"), P("hour", "region", None)),
        check_vma=False,
    )
```

```python
import jax
import jax.numpy as jnp
from jax import lax
from jax.experimental import pallas as pl
from jax.experimental.pallas import tpu as pltpu
from jax.sharding import PartitionSpec as P

BF16 = jnp.bfloat16
F32 = jnp.float32
I32 = jnp.int32
VMEM = pl.BlockSpec(memory_space=pltpu.VMEM)
HBM = pl.BlockSpec(memory_space=pltpu.HBM)
NT = (((1,), (1,)), ((), ()))
CHUNKS = 1
PARTNER = 2
RELAYED = (4, 1)
DIRECT = (7, 5)
LANES = 128
PARAMS = pltpu.CompilerParams(vmem_limit_bytes=16 * 1024 * 1024)


def swapped(value, axis, parity):
    count = lax.axis_size(axis)
    pairs = []
    for low in range(parity, count, 2):
        high = (low + 1) % count
        pairs += [(low, high), (high, low)]
    return lax.ppermute(value, axis, pairs)


def crossed(value, distance):
    count = lax.axis_size("region")
    return lax.ppermute(value, "region", [(i, i ^ distance) for i in range(count)])


def from_behind(value, axis):
    count = lax.axis_size(axis)
    return lax.ppermute(value, axis, [(i, (i + 1) % count) for i in range(count)])


def first_kernel(
    demand_in, matrix_in, bus_in, quad_in, lin_in, cap_in, ramp_in, start_in, count_in, part_in, share_in,
    angles_ref, inner_ref, outer_ref, edge_ref, matrix_ref, demand_ref, params_ref, slot_ref, part_ref, share_ref,
    bus_ref, quad_ref, lin_ref, cap_ref, ramp_ref, start_ref, count_ref, sems,
):
    buses = matrix_ref.shape[0]
    depth = buses // CHUNKS
    small = [
        (bus_in, bus_ref), (count_in, count_ref), (quad_in, quad_ref), (lin_in, lin_ref), (cap_in, cap_ref),
        (ramp_in, ramp_ref), (start_in, start_ref), (part_in, part_ref), (share_in, share_ref),
    ]
    demand_copy = pltpu.make_async_copy(demand_in, demand_ref, sems.at[0])
    demand_copy.start()
    copies = []
    for c in range(CHUNKS):
        rows = pl.ds(c * depth, depth)
        copies.append(pltpu.make_async_copy(matrix_in.at[rows], matrix_ref.at[rows], sems.at[1 + c]))
        copies[-1].start()
    small_copies = [
        pltpu.make_async_copy(source, target, sems.at[1 + CHUNKS + i]) for i, (source, target) in enumerate(small)
    ]
    for copy in small_copies:
        copy.start()
    for copy in small_copies:
        copy.wait()

    region = lax.axis_index("region")
    region_count = count_ref.shape[1]
    odd = lax.rem(region, 2)
    slots = bus_ref.shape[1]
    left_region = lax.rem(region + region_count - 1, region_count)
    regions = lax.broadcasted_iota(I32, count_ref.shape, 1)
    counts = count_ref[...]
    left_count = jnp.sum(jnp.where(regions == left_region, counts, 0), axis=1, keepdims=True)
    right_count = jnp.sum(jnp.where(regions == region, counts, 0), axis=1, keepdims=True)
    ids = lax.broadcasted_iota(I32, (1, slots), 1)
    left_bus = jnp.where(ids < left_count, bus_ref[0:1, :], -1)
    right_bus = jnp.where(ids < right_count, bus_ref[1:2, :], -1)
    inner_bus = jnp.where(odd == 0, right_bus, left_bus)
    outer_bus = jnp.where(odd == 0, left_bus, right_bus)
    slot_ref[...] = jnp.full(slot_ref.shape, -1, I32)
    slot_ref[0:1, :] = inner_bus
    slot_ref[1:2, :] = outer_bus
    params_ref[...] = jnp.zeros(params_ref.shape, F32)
    inverse = 1.0 / (quad_ref[...] + 1.0)
    params_ref[0:1, :] = inverse
    params_ref[1:2, :] = lin_ref[...]
    params_ref[2:3, :] = cap_ref[...]
    params_ref[3:4, :] = ramp_ref[...]
    params_ref[4:5, :] = start_ref[...]

    demand_copy.wait()
    right_side = demand_ref[...].astype(BF16)
    both_bus = jnp.concatenate([inner_bus, outer_bus], axis=1)
    ends = None
    for c in range(CHUNKS):
        rows = pl.ds(c * depth, depth)
        row_ids = lax.broadcasted_iota(I32, (depth, 2 * slots), 0) + c * depth
        one = (row_ids == both_bus).astype(F32).astype(BF16)
        copies[c].wait()
        part = lax.dot_general(right_side, matrix_ref[rows, :], NT, preferred_element_type=F32)
        angles_ref[:, rows] = part
        picked = jnp.dot(part.astype(BF16), one, preferred_element_type=F32)
        ends = picked if ends is None else ends + picked
    ends = ends.astype(BF16)
    inner_ref[...] = ends[:, :slots]
    outer_ref[...] = ends[:, slots:]
    hours = angles_ref.shape[0]
    tail = angles_ref[pl.ds(hours - 8, 8), :][7:8, :]
    target = (tail - lin_ref[...]) * inverse
    limited = jnp.minimum(jnp.maximum(target, -ramp_ref[...]), ramp_ref[...])
    edge_ref[...] = jnp.minimum(jnp.maximum(limited, 0.0), cap_ref[...])


def middle_kernel(
    angles_ref, demand_ref, matrix_ref, params_ref, slot_ref, part_ref, share_ref,
    base_ref, slot_matrix_ref, dual_ref, low_ref, high_ref, weight_ref,
):
    hours, buses = angles_ref.shape
    region = lax.axis_index("region")
    block = lax.axis_index("hour")
    inverse, lin, cap, ramp, start = (params_ref[i : i + 1, :] for i in range(5))
    angles = angles_ref[...]
    row = lax.broadcasted_iota(I32, (hours, buses), 0)
    first = jnp.logical_and(row == 0, block == 0)
    prior = jnp.where(first, jnp.broadcast_to(start, (hours, buses)), 0.0)
    target = (angles - lin) * inverse
    limited = jnp.minimum(jnp.maximum(target, prior - ramp), prior + ramp)
    generation = jnp.minimum(jnp.maximum(limited, 0.0), cap)
    dual = angles - generation
    dual_ref[...] = dual
    right_side = (demand_ref[...] + (generation - dual)).astype(BF16)
    before = pltpu.roll(generation, 1, 0)
    low_ref[...] = jnp.minimum(jnp.maximum(before - ramp, 0.0), cap)
    high_ref[...] = jnp.minimum(jnp.maximum(before + ramp, 0.0), cap)
    slots = slot_ref.shape[1]
    columns = jnp.transpose(slot_ref[...])
    lane = lax.broadcasted_iota(I32, (slots, buses), 1)
    picks = [(lane == columns[:, side : side + 1]).astype(F32).astype(BF16) for side in range(2)]
    stacked = jnp.concatenate([right_side] + picks, axis=0)
    product = lax.dot_general(stacked, matrix_ref[...], NT, preferred_element_type=F32)
    base_ref[...] = product[:hours]
    slot_matrix_ref[...] = product[hours:].astype(BF16)

    taps, parts = part_ref.shape
    local = part_ref[...] - region * buses
    inside = jnp.logical_and(local >= 0, local < buses)
    local = jnp.where(inside, local, -1)
    upper = lax.shift_right_arithmetic(local, 7)
    lower = jnp.where(inside, jnp.bitwise_and(local, LANES - 1), -1)
    share = share_ref[...]
    half = LANES // 2
    for group in range(parts // LANES):
        lanes = slice(group * LANES, (group + 1) * LANES)
        for part in range(2):
            ids = lax.broadcasted_iota(I32, (half, LANES), 0) + part * half
            values = [
                jnp.where(ids == lower[k : k + 1, lanes], share[k : k + 1, lanes], 0.0).astype(BF16) for k in range(taps)
            ]
            for a in range(buses // LANES):
                total = None
                for k in range(taps):
                    mask = jnp.where(upper[k : k + 1, lanes] == a, 1.0, 0.0)
                    mask = jnp.broadcast_to(mask, (half, LANES)).astype(BF16)
                    term = values[k] * mask
                    total = term if total is None else total + term
                weight_ref[a * LANES + part * half : a * LANES + (part + 1) * half, lanes] = total


def last_kernel(
    base_ref, slot_matrix_ref, outer_ref, inner_ref, edge_ref, dual_ref, low_ref, high_ref, weight_ref, params_ref,
    angles_out, *rest,
):
    *piece_refs, price_ref, angles_ref, sem = rest
    hours, buses = base_ref.shape
    slots = inner_ref.shape[1]
    block = lax.axis_index("hour")
    inverse, lin, cap, ramp, start = (params_ref[i : i + 1, :] for i in range(5))
    far = jnp.concatenate([inner_ref[...], outer_ref[...]], axis=1)
    angles = base_ref[...] + jnp.dot(far, slot_matrix_ref[...], preferred_element_type=F32)
    angles_ref[...] = angles
    copy = pltpu.make_async_copy(angles_ref, angles_out, sem)
    copy.start()
    prior = jnp.where(block == 0, start, edge_ref[...])
    low_first = jnp.minimum(jnp.maximum(prior - ramp, 0.0), cap)
    high_first = jnp.minimum(jnp.maximum(prior + ramp, 0.0), cap)
    first = lax.broadcasted_iota(I32, (hours, buses), 0) == 0
    low = jnp.where(first, low_first, low_ref[...])
    high = jnp.where(first, high_first, high_ref[...])
    total = angles + dual_ref[...]
    target = (total - lin) * inverse
    generation = jnp.minimum(jnp.maximum(target, low), high)
    lmp = (total - generation).astype(BF16)
    price_ref[...] = jnp.dot(lmp, weight_ref[...], preferred_element_type=F32).astype(BF16)
    region = lax.axis_index("region")
    if piece_refs:
        kept_ref, passed_ref, *direct_refs = piece_refs
        rows = direct_refs[0].shape[0]

        def piece(k):
            owner = jnp.bitwise_xor(region, k)
            return price_ref[pl.ds(pl.multiple_of(owner * rows, rows), rows), :]

        for i, k in enumerate((0,) + RELAYED):
            kept_ref[i * rows : (i + 1) * rows, :] = piece(k)
            passed_ref[i * rows : (i + 1) * rows, :] = piece(k ^ PARTNER)
        for k, direct_ref in zip(DIRECT, direct_refs):
            direct_ref[...] = piece(k)
    copy.wait()


def relay_kernel(kept_ref, got_ref, *sum_refs):
    rows = sum_refs[0].shape[0]
    for i, sum_ref in enumerate(sum_refs):
        part = slice(i * rows, (i + 1) * rows)
        total = kept_ref[part, :].astype(F32) + got_ref[part, :].astype(F32)
        sum_ref[...] = total.astype(sum_ref.dtype)


def pay_kernel(cleared_ref, *refs):
    *piece_refs, out_ref = refs
    total = piece_refs[0][...].astype(F32)
    for piece_ref in piece_refs[1:]:
        total = total + piece_ref[...].astype(F32)
    out_ref[...] = cleared_ref[...] * total


def shards(
    kkt_inverse, demand, cost_quad, cost_lin, capacity, ramp, gen_start, boundary_bus, tie_count,
    part_bus, part_share, cleared_mw,
):
    region_count = lax.axis_size("region")
    hours, buses = demand.shape
    slots = boundary_bus.shape[2]
    parts, taps = part_bus.shape
    rows = [v.reshape(1, buses) for v in (cost_quad, cost_lin, capacity, ramp, gen_start)]
    wide = jax.ShapeDtypeStruct((hours, buses), F32)
    row = jax.ShapeDtypeStruct((1, buses), F32)
    square = jax.ShapeDtypeStruct((buses, buses), BF16)
    ends = jax.ShapeDtypeStruct((hours, slots), BF16)
    angles, inner, outer, edge, matrix, demand, params, slot_bus, part_bus, part_share = pl.pallas_call(
        first_kernel,
        out_shape=(
            wide, ends, ends, row, square, wide,
            jax.ShapeDtypeStruct((8, buses), F32),
            jax.ShapeDtypeStruct((8, slots), I32),
            jax.ShapeDtypeStruct((taps, parts), I32),
            jax.ShapeDtypeStruct((taps, parts), F32),
        ),
        in_specs=[HBM] * 11,
        out_specs=(VMEM,) * 10,
        scratch_shapes=[pltpu.VMEM((2, slots), I32)]
        + [pltpu.VMEM((1, buses), F32)] * 5
        + [pltpu.VMEM((1, region_count), I32), pltpu.SemaphoreType.DMA((CHUNKS + 10,))],
        compiler_params=PARAMS,
        name="first_angles",
    )(
        *(
            pltpu.with_memory_space_constraint(v, pltpu.HBM)
            for v in (
                demand, kkt_inverse[0], boundary_bus[0], *rows, tie_count.reshape(1, region_count),
                part_bus.T, part_share.T,
            )
        )
    )
    outer = swapped(outer, "region", 1)
    inner = swapped(inner, "region", 0)
    edge = from_behind(edge, "hour")
    base, slot_matrix, dual, low, high, weight = pl.pallas_call(
        middle_kernel,
        out_shape=(
            wide,
            jax.ShapeDtypeStruct((2 * slots, buses), BF16),
            wide,
            wide,
            wide,
            jax.ShapeDtypeStruct((buses, parts), BF16),
        ),
        in_specs=[VMEM] * 7,
        out_specs=(VMEM,) * 6,
        compiler_params=PARAMS,
        cost_estimate=pl.CostEstimate(flops=2 * 384 * buses * buses, bytes_accessed=12 << 20, transcendentals=0),
        name="middle",
    )(angles, demand, matrix, params, slot_bus, part_bus, part_share)
    own_hours = hours // region_count
    price_shape = jax.ShapeDtypeStruct((hours, parts), BF16)
    direct = own_hours % 16 == 0 and region_count == 8
    price_buffer = [pltpu.VMEM((hours, parts), BF16)] if direct else []
    piece = jax.ShapeDtypeStruct((own_hours, parts), BF16)
    relayed = jax.ShapeDtypeStruct((own_hours * (1 + len(RELAYED)), parts), BF16)
    price_out = [relayed, relayed] + [piece] * len(DIRECT) if direct else [price_shape]
    angles, *price = pl.pallas_call(
        last_kernel,
        out_shape=(wide, *price_out),
        in_specs=[VMEM] * 10,
        out_specs=(HBM,) + (VMEM,) * len(price_out),
        scratch_shapes=price_buffer + [pltpu.VMEM((hours, buses), F32), pltpu.SemaphoreType.DMA],
        compiler_params=PARAMS,
        name="second_angles",
    )(base, slot_matrix, outer, inner, edge, dual, low, high, weight, params)
    if direct:
        kept, passed, *straight = price
        passed = crossed(passed, PARTNER)
        straight = [crossed(v, k) for v, k in zip(straight, DIRECT)]
        own, *sums = pl.pallas_call(
            relay_kernel,
            out_shape=(jax.ShapeDtypeStruct((own_hours, parts), F32),) + (piece,) * len(RELAYED),
            in_specs=[VMEM] * 2,
            out_specs=(VMEM,) * (1 + len(RELAYED)),
            compiler_params=PARAMS,
            name="relay",
        )(kept, passed)
        pieces = [own] + [crossed(v, k) for v, k in zip(sums, RELAYED)] + straight
    else:
        pieces = lax.all_to_all(price[0].reshape(region_count, own_hours, parts), "region", 0, 0, tiled=True)
        pieces = [pieces[i] for i in range(region_count)]
    payment = pl.pallas_call(
        pay_kernel,
        out_shape=jax.ShapeDtypeStruct(cleared_mw.shape[1:], F32),
        in_specs=[VMEM] * (1 + len(pieces)),
        out_specs=VMEM,
        compiler_params=PARAMS,
        name="payment",
    )(cleared_mw[0], *pieces)
    return angles, payment[None]


def solution(mesh):
    return jax.shard_map(
        shards,
        mesh=mesh,
        in_specs=(
            P("region", None, None),
            P("hour", "region"),
            P("region"),
            P("region"),
            P("region"),
            P("region"),
            P("region"),
            P("region", None, None),
            P(),
            P(),
            P(),
            P("hour", "region", None),
        ),
        out_specs=(P("hour", "region"), P("hour", "region", None)),
        check_vma=False,
    )
```

```python
import functools

import jax
import jax.numpy as jnp
from jax import lax
from jax.experimental import pallas as pl
from jax.experimental.pallas import tpu as pltpu
from jax.sharding import PartitionSpec as P

BF16 = jnp.bfloat16
F32 = jnp.float32
I32 = jnp.int32
VMEM = pl.BlockSpec(memory_space=pltpu.VMEM)
HBM = pl.BlockSpec(memory_space=pltpu.HBM)
NT = (((1,), (1,)), ((), ()))
TN = (((0,), (0,)), ((), ()))
FIRST = {2: (4,), 1: (4,), 7: (), 3: ()}
SECOND = {4: (2, 1)}
LANES = 128
EARLY = 2
PARAMS = pltpu.CompilerParams(vmem_limit_bytes=16 * 1024 * 1024)


def in_hbm(*arrays):
    return [pltpu.with_memory_space_constraint(v, pltpu.HBM) for v in arrays]


def swapped(value, axis, parity):
    count = lax.axis_size(axis)
    pairs = []
    for low in range(parity, count, 2):
        high = (low + 1) % count
        pairs += [(low, high), (high, low)]
    return lax.ppermute(value, axis, pairs)


def crossed(value, step):
    return lax.ppermute(value, "region", [(i, i ^ step) for i in range(lax.axis_size("region"))])


def from_behind(value, axis):
    count = lax.axis_size(axis)
    return lax.ppermute(value, axis, [(i, (i + 1) % count) for i in range(count)])


def shares_by_bus(part_ref, share_ref, weight_ref, region, begin, end):
    buses = weight_ref.shape[0]
    taps = part_ref.shape[0]
    local = part_ref[...] - region * buses
    inside = jnp.logical_and(local >= 0, local < buses)
    local = jnp.where(inside, local, -1)
    upper = lax.shift_right_arithmetic(local, 7)
    lower = jnp.where(inside, jnp.bitwise_and(local, LANES - 1), -1)
    share = share_ref[...]
    half = LANES // 2
    for group in range(begin, end):
        lanes = slice(group * LANES, (group + 1) * LANES)
        out_lanes = slice((group - begin) * LANES, (group - begin + 1) * LANES)
        for part in range(2):
            ids = lax.broadcasted_iota(I32, (half, LANES), 0) + part * half
            values = [
                jnp.where(ids == lower[k : k + 1, lanes], share[k : k + 1, lanes], 0.0).astype(BF16) for k in range(taps)
            ]
            for a in range(buses // LANES):
                total = None
                for k in range(taps):
                    mask = jnp.where(upper[k : k + 1, lanes] == a, 1.0, 0.0)
                    mask = jnp.broadcast_to(mask, (half, LANES)).astype(BF16)
                    term = values[k] * mask
                    total = term if total is None else total + term
                weight_ref[a * LANES + part * half : a * LANES + (part + 1) * half, out_lanes] = total


def ends_kernel(
    demand_in, matrix_in, bus_in, count_in, part_in, share_in,
    inner_ref, outer_ref, matrix_ref, demand_ref, pick_ref, part_ref, share_ref, weight_ref,
    bus_ref, count_ref, sems,
):
    buses = matrix_ref.shape[0]
    copies = [
        pltpu.make_async_copy(source, target, sems.at[i])
        for i, (source, target) in enumerate(
            [
                (bus_in, bus_ref), (count_in, count_ref), (part_in, part_ref), (share_in, share_ref),
                (demand_in, demand_ref), (matrix_in, matrix_ref),
            ]
        )
    ]
    for copy in copies:
        copy.start()
    for copy in copies[:4]:
        copy.wait()

    region = lax.axis_index("region")
    region_count = count_ref.shape[1]
    odd = lax.rem(region, 2)
    slots = bus_ref.shape[1]
    left_region = lax.rem(region + region_count - 1, region_count)
    regions = lax.broadcasted_iota(I32, count_ref.shape, 1)
    counts = count_ref[...]
    left_count = jnp.sum(jnp.where(regions == left_region, counts, 0), axis=1, keepdims=True)
    right_count = jnp.sum(jnp.where(regions == region, counts, 0), axis=1, keepdims=True)
    ids = lax.broadcasted_iota(I32, (1, slots), 1)
    left_bus = jnp.where(ids < left_count, bus_ref[0:1, :], -1)
    right_bus = jnp.where(ids < right_count, bus_ref[1:2, :], -1)
    inner_bus = jnp.where(odd == 0, right_bus, left_bus)
    outer_bus = jnp.where(odd == 0, left_bus, right_bus)
    columns = jnp.transpose(jnp.concatenate([inner_bus, outer_bus] * 4, axis=0))
    lane = lax.broadcasted_iota(I32, (slots, buses), 1)
    for side in range(2):
        pick = (lane == columns[:, side : side + 1]).astype(F32).astype(BF16)
        pick_ref[side * slots : (side + 1) * slots, :] = pick
    shares_by_bus(part_ref, share_ref, weight_ref, region, 0, EARLY)
    copies[4].wait()
    right_side = jnp.transpose(demand_ref[...]).astype(BF16)
    copies[5].wait()
    slot_rows = jnp.dot(pick_ref[...], matrix_ref[...], preferred_element_type=F32).astype(BF16)
    ends = jnp.dot(slot_rows, right_side, preferred_element_type=F32).astype(BF16)
    inner_ref[...] = ends[:slots]
    outer_ref[...] = ends[slots:]


def edge_kernel(
    demand_ref, matrix_ref, quad_ref, lin_ref, cap_ref, ramp_ref, start_ref,
    angles_ref, edge_ref, params_ref,
):
    hours, buses = demand_ref.shape
    angles = lax.dot_general(demand_ref[...].astype(BF16), matrix_ref[...], NT, preferred_element_type=F32)
    angles_ref[...] = angles
    inverse, lin, cap, ramp = 1.0 / (quad_ref[...] + 1.0), lin_ref[...], cap_ref[...], ramp_ref[...]
    pad = jnp.zeros((3, buses), F32)
    params_ref[...] = jnp.concatenate([inverse, lin, cap, ramp, start_ref[...], pad], axis=0)
    target = (angles[hours - 1 :, :] - lin) * inverse
    limited = jnp.minimum(jnp.maximum(target, -ramp), ramp)
    edge_ref[...] = jnp.minimum(jnp.maximum(limited, 0.0), cap)


def middle_kernel(
    angles_ref, demand_ref, params_ref, pick_ref, matrix_ref, part_ref, share_ref,
    base_ref, slot_matrix_ref, dual_ref, low_ref, high_ref, weight_ref,
):
    hours, buses = demand_ref.shape
    region = lax.axis_index("region")
    block = lax.axis_index("hour")
    inverse, lin, cap, ramp, start = (params_ref[i : i + 1, :] for i in range(5))
    angles = angles_ref[...]
    row = lax.broadcasted_iota(I32, (hours, buses), 0)
    first = jnp.logical_and(row == 0, block == 0)
    prior = jnp.where(first, jnp.broadcast_to(start, (hours, buses)), 0.0)
    target = (angles - lin) * inverse
    limited = jnp.minimum(jnp.maximum(target, prior - ramp), prior + ramp)
    generation = jnp.minimum(jnp.maximum(limited, 0.0), cap)
    dual = angles - generation
    dual_ref[...] = dual
    right_side = (demand_ref[...] + (generation - dual)).astype(BF16)
    before = pltpu.roll(generation, 1, 0)
    low_ref[...] = jnp.minimum(jnp.maximum(before - ramp, 0.0), cap)
    high_ref[...] = jnp.minimum(jnp.maximum(before + ramp, 0.0), cap)
    stacked = jnp.concatenate([right_side, pick_ref[...]], axis=0)
    product = lax.dot_general(stacked, matrix_ref[...], NT, preferred_element_type=F32)
    base_ref[...] = product[:hours]
    slot_matrix_ref[...] = product[hours:].astype(BF16)
    shares_by_bus(part_ref, share_ref, weight_ref, region, EARLY, part_ref.shape[1] // LANES)


def last_kernel(
    base_ref, slot_matrix_ref, outer_ref, inner_ref, edge_ref, dual_ref, low_ref, high_ref, early_ref, weight_ref, params_ref,
    angles_ref, *rest,
):
    *piece_refs, price_ref = rest
    hours, buses = base_ref.shape
    block = lax.axis_index("hour")
    inverse, lin, cap, ramp, start = (params_ref[i : i + 1, :] for i in range(5))
    far = jnp.concatenate([inner_ref[...], outer_ref[...]], axis=0)
    angles = base_ref[...] + lax.dot_general(far, slot_matrix_ref[...], TN, preferred_element_type=F32)
    angles_ref[...] = angles
    prior = jnp.where(block == 0, start, edge_ref[...])
    low_first = jnp.minimum(jnp.maximum(prior - ramp, 0.0), cap)
    high_first = jnp.minimum(jnp.maximum(prior + ramp, 0.0), cap)
    first = lax.broadcasted_iota(I32, (hours, buses), 0) == 0
    low = jnp.where(first, low_first, low_ref[...])
    high = jnp.where(first, high_first, high_ref[...])
    total = angles + dual_ref[...]
    target = (total - lin) * inverse
    generation = jnp.minimum(jnp.maximum(target, low), high)
    lmp = (total - generation).astype(BF16)
    cut = early_ref.shape[1]
    price_ref[:, :cut] = jnp.dot(lmp, early_ref[...], preferred_element_type=F32).astype(BF16)
    price_ref[:, cut:] = jnp.dot(lmp, weight_ref[...], preferred_element_type=F32).astype(BF16)
    region = lax.axis_index("region")
    if piece_refs:
        rows = piece_refs[0].shape[0]

        def piece(step):
            owner = jnp.bitwise_xor(region, step)
            return price_ref[pl.ds(pl.multiple_of(owner * rows, rows), rows), :]

        kept = [0] + list(SECOND)
        for step, kept_ref in zip(kept, piece_refs):
            kept_ref[...] = piece(step)
        for (step, relays), sent_ref in zip(FIRST.items(), piece_refs[len(kept) :]):
            for i, k in enumerate([step] + [step ^ relay for relay in relays]):
                sent_ref[i * rows : (i + 1) * rows, :] = piece(k)


def relay_kernel(places, kept_ref, *refs):
    *got_refs, sum_ref = refs
    rows = kept_ref.shape[0]
    total = kept_ref[...].astype(F32)
    for place, got_ref in zip(places, got_refs):
        total = total + got_ref[place * rows : (place + 1) * rows, :].astype(F32)
    sum_ref[...] = total.astype(BF16)


def store_kernel(angles_ref, after_ref, angles_out, sem):
    copy = pltpu.make_async_copy(angles_ref, angles_out, sem)
    copy.start()
    copy.wait()


def pay_kernel(cleared_ref, *refs):
    *piece_refs, out_ref = refs
    rows = out_ref.shape[0]
    total = piece_refs[0][:rows, :].astype(F32)
    for piece_ref in piece_refs[1:]:
        total = total + piece_ref[:rows, :].astype(F32)
    out_ref[...] = cleared_ref[...] * total


def shards(
    kkt_inverse, demand, cost_quad, cost_lin, capacity, ramp, gen_start, boundary_bus, tie_count,
    part_bus, part_share, cleared_mw,
):
    region_count = lax.axis_size("region")
    hours, buses = demand.shape
    slots = boundary_bus.shape[2]
    parts, taps = part_bus.shape
    rows = [v.reshape(1, buses) for v in (cost_quad, cost_lin, capacity, ramp, gen_start)]
    wide = jax.ShapeDtypeStruct((hours, buses), F32)
    row = jax.ShapeDtypeStruct((1, buses), F32)
    square = jax.ShapeDtypeStruct((buses, buses), BF16)
    ends = jax.ShapeDtypeStruct((slots, hours), BF16)
    table = jax.ShapeDtypeStruct((8, buses), F32)
    inner, outer, matrix, demand, pick, part_bus, part_share, early = pl.pallas_call(
        ends_kernel,
        out_shape=(
            ends, ends, square, wide,
            jax.ShapeDtypeStruct((2 * slots, buses), BF16),
            jax.ShapeDtypeStruct((taps, parts), I32),
            jax.ShapeDtypeStruct((taps, parts), F32),
            jax.ShapeDtypeStruct((buses, EARLY * LANES), BF16),
        ),
        in_specs=[HBM] * 6,
        out_specs=(VMEM,) * 8,
        scratch_shapes=[
            pltpu.VMEM((2, slots), I32),
            pltpu.VMEM((1, region_count), I32),
            pltpu.SemaphoreType.DMA((6,)),
        ],
        compiler_params=PARAMS,
        name="ends",
    )(*in_hbm(demand, kkt_inverse[0], boundary_bus[0], tie_count.reshape(1, region_count), part_bus.T, part_share.T))
    outer = swapped(outer, "region", 1)
    inner = swapped(inner, "region", 0)
    angles, edge, params = pl.pallas_call(
        edge_kernel,
        out_shape=(wide, row, table),
        in_specs=[VMEM] * 7,
        out_specs=(VMEM,) * 3,
        compiler_params=PARAMS,
        cost_estimate=pl.CostEstimate(flops=2 * hours * buses * buses, bytes_accessed=4 << 20, transcendentals=0),
        name="edge",
    )(demand, matrix, *rows)
    edge = from_behind(edge, "hour")
    base, slot_matrix, dual, low, high, weight = pl.pallas_call(
        middle_kernel,
        out_shape=(
            wide,
            jax.ShapeDtypeStruct((2 * slots, buses), BF16),
            wide,
            wide,
            wide,
            jax.ShapeDtypeStruct((buses, parts - EARLY * LANES), BF16),
        ),
        in_specs=[VMEM] * 7,
        out_specs=(VMEM,) * 6,
        compiler_params=PARAMS,
        cost_estimate=pl.CostEstimate(flops=2 * 384 * buses * buses, bytes_accessed=12 << 20, transcendentals=0),
        name="middle",
    )(angles, demand, params, pick, matrix, part_bus, part_share)
    own_hours = hours // region_count
    price_shape = jax.ShapeDtypeStruct((hours, parts), BF16)
    direct = own_hours % 16 == 0 and region_count == 8
    price_buffer = [pltpu.VMEM((hours, parts), BF16)] if direct else []
    piece = jax.ShapeDtypeStruct((own_hours, parts), BF16)
    price_out = [price_shape]
    if direct:
        price_out = [piece] * (1 + len(SECOND)) + [
            jax.ShapeDtypeStruct((own_hours * (1 + len(relays)), parts), BF16) for relays in FIRST.values()
        ]
    angles, *price = pl.pallas_call(
        last_kernel,
        out_shape=(wide, *price_out),
        in_specs=[VMEM] * 11,
        out_specs=(VMEM,) * (1 + len(price_out)),
        scratch_shapes=price_buffer,
        compiler_params=PARAMS,
        name="second_angles",
    )(base, slot_matrix, outer, inner, edge, dual, low, high, early, weight, params)
    if direct:
        own, *price = price
        kept = dict(zip(SECOND, price))
        got = {step: crossed(v, step) for step, v in zip(FIRST, price[len(SECOND) :])}
        sums = []
        for step, sources in SECOND.items():
            places = [1 + FIRST[source].index(step) for source in sources]
            total = pl.pallas_call(
                functools.partial(relay_kernel, places),
                out_shape=piece,
                in_specs=[VMEM] * (1 + len(sources)),
                out_specs=VMEM,
                compiler_params=PARAMS,
                name="relay",
            )(kept[step], *(got[source] for source in sources))
            sums.append(crossed(total, step))
        pieces = [own] + list(got.values()) + sums
        after = total
    else:
        pieces = lax.all_to_all(price[0].reshape(region_count, own_hours, parts), "region", 0, 0, tiled=True)
        pieces = [pieces[i] for i in range(region_count)]
        after = pieces[0]
    angles = pl.pallas_call(
        store_kernel,
        out_shape=wide,
        in_specs=[VMEM, VMEM],
        out_specs=HBM,
        scratch_shapes=[pltpu.SemaphoreType.DMA],
        compiler_params=PARAMS,
        cost_estimate=pl.CostEstimate(flops=0, bytes_accessed=8 * hours * buses, transcendentals=0),
        name="store",
    )(angles, after)
    payment = pl.pallas_call(
        pay_kernel,
        out_shape=jax.ShapeDtypeStruct(cleared_mw.shape[1:], F32),
        in_specs=[VMEM] * (1 + len(pieces)),
        out_specs=VMEM,
        compiler_params=PARAMS,
        name="payment",
    )(cleared_mw[0], *pieces)
    return angles, payment[None]


def solution(mesh):
    return jax.shard_map(
        shards,
        mesh=mesh,
        in_specs=(
            P("region", None, None),
            P("hour", "region"),
            P("region"),
            P("region"),
            P("region"),
            P("region"),
            P("region"),
            P("region", None, None),
            P(),
            P(),
            P(),
            P("hour", "region", None),
        ),
        out_specs=(P("hour", "region"), P("hour", "region", None)),
        check_vma=False,
    )
```

```python
import functools

import jax
import jax.numpy as jnp
from jax import lax
from jax.experimental import pallas as pl
from jax.experimental.pallas import tpu as pltpu
from jax.sharding import PartitionSpec as P

BF16 = jnp.bfloat16
F32 = jnp.float32
I32 = jnp.int32
VMEM = pl.BlockSpec(memory_space=pltpu.VMEM)
HBM = pl.BlockSpec(memory_space=pltpu.HBM)
NT = (((1,), (1,)), ((), ()))
TN = (((0,), (0,)), ((), ()))
FIRST = {2: (4,), 1: (4,), 7: (), 3: ()}
SECOND = {4: (2, 1)}
LANES = 128
EARLY = 2
PARAMS = pltpu.CompilerParams(vmem_limit_bytes=16 * 1024 * 1024)


def in_hbm(*arrays):
    return [pltpu.with_memory_space_constraint(v, pltpu.HBM) for v in arrays]


def swapped(value, axis, parity):
    count = lax.axis_size(axis)
    pairs = []
    for low in range(parity, count, 2):
        high = (low + 1) % count
        pairs += [(low, high), (high, low)]
    return lax.ppermute(value, axis, pairs)


def crossed(value, step):
    return lax.ppermute(value, "region", [(i, i ^ step) for i in range(lax.axis_size("region"))])


def from_behind(value, axis):
    count = lax.axis_size(axis)
    return lax.ppermute(value, axis, [(i, (i + 1) % count) for i in range(count)])


def shares_by_bus(part_ref, share_ref, weight_ref, region, begin, end):
    buses = weight_ref.shape[0]
    taps = part_ref.shape[0]
    local = part_ref[...] - region * buses
    inside = jnp.logical_and(local >= 0, local < buses)
    local = jnp.where(inside, local, -1)
    upper = lax.shift_right_arithmetic(local, 7)
    lower = jnp.where(inside, jnp.bitwise_and(local, LANES - 1), -1)
    share = share_ref[...]
    half = LANES // 2
    for group in range(begin, end):
        lanes = slice(group * LANES, (group + 1) * LANES)
        out_lanes = slice((group - begin) * LANES, (group - begin + 1) * LANES)
        for part in range(2):
            ids = lax.broadcasted_iota(I32, (half, LANES), 0) + part * half
            values = [
                jnp.where(ids == lower[k : k + 1, lanes], share[k : k + 1, lanes], 0.0).astype(BF16) for k in range(taps)
            ]
            for a in range(buses // LANES):
                total = None
                for k in range(taps):
                    mask = jnp.where(upper[k : k + 1, lanes] == a, 1.0, 0.0)
                    mask = jnp.broadcast_to(mask, (half, LANES)).astype(BF16)
                    term = values[k] * mask
                    total = term if total is None else total + term
                weight_ref[a * LANES + part * half : a * LANES + (part + 1) * half, out_lanes] = total


def ends_kernel(
    demand_in, matrix_in, bus_in, count_in, part_in, share_in,
    inner_ref, outer_ref, matrix_ref, demand_ref, pick_ref, part_ref, share_ref, weight_ref,
    bus_ref, count_ref, sems,
):
    buses = matrix_ref.shape[0]
    copies = [
        pltpu.make_async_copy(source, target, sems.at[i])
        for i, (source, target) in enumerate(
            [
                (bus_in, bus_ref), (count_in, count_ref), (part_in, part_ref), (share_in, share_ref),
                (demand_in, demand_ref), (matrix_in, matrix_ref),
            ]
        )
    ]
    for copy in copies:
        copy.start()
    for copy in copies[:4]:
        copy.wait()

    region = lax.axis_index("region")
    region_count = count_ref.shape[1]
    odd = lax.rem(region, 2)
    slots = bus_ref.shape[1]
    left_region = lax.rem(region + region_count - 1, region_count)
    regions = lax.broadcasted_iota(I32, count_ref.shape, 1)
    counts = count_ref[...]
    left_count = jnp.sum(jnp.where(regions == left_region, counts, 0), axis=1, keepdims=True)
    right_count = jnp.sum(jnp.where(regions == region, counts, 0), axis=1, keepdims=True)
    ids = lax.broadcasted_iota(I32, (1, slots), 1)
    left_bus = jnp.where(ids < left_count, bus_ref[0:1, :], -1)
    right_bus = jnp.where(ids < right_count, bus_ref[1:2, :], -1)
    inner_bus = jnp.where(odd == 0, right_bus, left_bus)
    outer_bus = jnp.where(odd == 0, left_bus, right_bus)
    columns = jnp.transpose(jnp.concatenate([inner_bus, outer_bus] * 4, axis=0))
    lane = lax.broadcasted_iota(I32, (slots, buses), 1)
    for side in range(2):
        pick = (lane == columns[:, side : side + 1]).astype(F32).astype(BF16)
        pick_ref[side * slots : (side + 1) * slots, :] = pick
    shares_by_bus(part_ref, share_ref, weight_ref, region, 0, EARLY)
    copies[4].wait()
    right_side = jnp.transpose(demand_ref[...]).astype(BF16)
    copies[5].wait()
    slot_rows = jnp.dot(pick_ref[...], matrix_ref[...], preferred_element_type=F32).astype(BF16)
    ends = jnp.dot(slot_rows, right_side, preferred_element_type=F32).astype(BF16)
    inner_ref[...] = ends[:slots]
    outer_ref[...] = ends[slots:]


def edge_kernel(
    demand_ref, pick_ref, matrix_ref, quad_ref, lin_ref, cap_ref, ramp_ref, start_ref,
    stacked_ref, edge_ref, params_ref,
):
    hours, buses = demand_ref.shape
    stacked_ref[:hours, :] = demand_ref[...].astype(BF16)
    stacked_ref[hours:, :] = pick_ref[...]
    tail = demand_ref[pl.ds(hours - 16, 16), :].astype(BF16)
    angles = lax.dot_general(tail, matrix_ref[...], NT, preferred_element_type=F32)[15:]
    inverse, lin, cap, ramp = 1.0 / (quad_ref[...] + 1.0), lin_ref[...], cap_ref[...], ramp_ref[...]
    pad = jnp.zeros((3, buses), F32)
    params_ref[...] = jnp.concatenate([inverse, lin, cap, ramp, start_ref[...], pad], axis=0)
    target = (angles - lin) * inverse
    limited = jnp.minimum(jnp.maximum(target, -ramp), ramp)
    edge_ref[...] = jnp.minimum(jnp.maximum(limited, 0.0), cap)


def middle_kernel(
    stacked_ref, demand_ref, params_ref, matrix_ref, part_ref, share_ref,
    base_ref, slot_matrix_ref, dual_ref, low_ref, high_ref, weight_ref,
):
    hours, buses = demand_ref.shape
    region = lax.axis_index("region")
    block = lax.axis_index("hour")
    inverse, lin, cap, ramp, start = (params_ref[i : i + 1, :] for i in range(5))
    demand = demand_ref[...]
    product = lax.dot_general(stacked_ref[...], matrix_ref[...], NT, preferred_element_type=F32)
    slot_matrix_ref[...] = product[hours:].astype(BF16)
    angles = product[:hours]
    row = lax.broadcasted_iota(I32, (hours, buses), 0)
    first = jnp.logical_and(row == 0, block == 0)
    prior = jnp.where(first, jnp.broadcast_to(start, (hours, buses)), 0.0)
    target = (angles - lin) * inverse
    limited = jnp.minimum(jnp.maximum(target, prior - ramp), prior + ramp)
    generation = jnp.minimum(jnp.maximum(limited, 0.0), cap)
    dual = angles - generation
    dual_ref[...] = dual
    right_side = (demand + (generation - dual)).astype(BF16)
    before = pltpu.roll(generation, 1, 0)
    low_ref[...] = jnp.minimum(jnp.maximum(before - ramp, 0.0), cap)
    high_ref[...] = jnp.minimum(jnp.maximum(before + ramp, 0.0), cap)
    base_ref[...] = lax.dot_general(right_side, matrix_ref[...], NT, preferred_element_type=F32)
    shares_by_bus(part_ref, share_ref, weight_ref, region, EARLY, part_ref.shape[1] // LANES)


def last_kernel(
    base_ref, slot_matrix_ref, outer_ref, inner_ref, edge_ref, dual_ref, low_ref, high_ref, early_ref, weight_ref, params_ref,
    angles_ref, *rest,
):
    *piece_refs, price_ref = rest
    hours, buses = base_ref.shape
    block = lax.axis_index("hour")
    inverse, lin, cap, ramp, start = (params_ref[i : i + 1, :] for i in range(5))
    far = jnp.concatenate([inner_ref[...], outer_ref[...]], axis=0)
    angles = base_ref[...] + lax.dot_general(far, slot_matrix_ref[...], TN, preferred_element_type=F32)
    angles_ref[...] = angles
    prior = jnp.where(block == 0, start, edge_ref[...])
    low_first = jnp.minimum(jnp.maximum(prior - ramp, 0.0), cap)
    high_first = jnp.minimum(jnp.maximum(prior + ramp, 0.0), cap)
    first = lax.broadcasted_iota(I32, (hours, buses), 0) == 0
    low = jnp.where(first, low_first, low_ref[...])
    high = jnp.where(first, high_first, high_ref[...])
    total = angles + dual_ref[...]
    target = (total - lin) * inverse
    generation = jnp.minimum(jnp.maximum(target, low), high)
    lmp = (total - generation).astype(BF16)
    cut = early_ref.shape[1]
    price_ref[:, :cut] = jnp.dot(lmp, early_ref[...], preferred_element_type=F32).astype(BF16)
    price_ref[:, cut:] = jnp.dot(lmp, weight_ref[...], preferred_element_type=F32).astype(BF16)
    region = lax.axis_index("region")
    if piece_refs:
        rows = piece_refs[0].shape[0]

        def piece(step):
            owner = jnp.bitwise_xor(region, step)
            return price_ref[pl.ds(pl.multiple_of(owner * rows, rows), rows), :]

        kept = [0] + list(SECOND)
        for step, kept_ref in zip(kept, piece_refs):
            kept_ref[...] = piece(step)
        for (step, relays), sent_ref in zip(FIRST.items(), piece_refs[len(kept) :]):
            for i, k in enumerate([step] + [step ^ relay for relay in relays]):
                sent_ref[i * rows : (i + 1) * rows, :] = piece(k)


def relay_kernel(places, kept_ref, *refs):
    *got_refs, sum_ref = refs
    rows = kept_ref.shape[0]
    total = kept_ref[...].astype(F32)
    for place, got_ref in zip(places, got_refs):
        total = total + got_ref[place * rows : (place + 1) * rows, :].astype(F32)
    sum_ref[...] = total.astype(BF16)


def store_kernel(angles_ref, after_ref, angles_out, sem):
    copy = pltpu.make_async_copy(angles_ref, angles_out, sem)
    copy.start()
    copy.wait()


def pay_kernel(cleared_ref, *refs):
    *piece_refs, out_ref = refs
    rows = out_ref.shape[0]
    total = piece_refs[0][:rows, :].astype(F32)
    for piece_ref in piece_refs[1:]:
        total = total + piece_ref[:rows, :].astype(F32)
    out_ref[...] = cleared_ref[...] * total


def shards(
    kkt_inverse, demand, cost_quad, cost_lin, capacity, ramp, gen_start, boundary_bus, tie_count,
    part_bus, part_share, cleared_mw,
):
    region_count = lax.axis_size("region")
    hours, buses = demand.shape
    slots = boundary_bus.shape[2]
    parts, taps = part_bus.shape
    rows = [v.reshape(1, buses) for v in (cost_quad, cost_lin, capacity, ramp, gen_start)]
    wide = jax.ShapeDtypeStruct((hours, buses), F32)
    row = jax.ShapeDtypeStruct((1, buses), F32)
    square = jax.ShapeDtypeStruct((buses, buses), BF16)
    ends = jax.ShapeDtypeStruct((slots, hours), BF16)
    table = jax.ShapeDtypeStruct((8, buses), F32)
    inner, outer, matrix, demand, pick, part_bus, part_share, early = pl.pallas_call(
        ends_kernel,
        out_shape=(
            ends, ends, square, wide,
            jax.ShapeDtypeStruct((2 * slots, buses), BF16),
            jax.ShapeDtypeStruct((taps, parts), I32),
            jax.ShapeDtypeStruct((taps, parts), F32),
            jax.ShapeDtypeStruct((buses, EARLY * LANES), BF16),
        ),
        in_specs=[HBM] * 6,
        out_specs=(VMEM,) * 8,
        scratch_shapes=[
            pltpu.VMEM((2, slots), I32),
            pltpu.VMEM((1, region_count), I32),
            pltpu.SemaphoreType.DMA((6,)),
        ],
        compiler_params=PARAMS,
        name="ends",
    )(*in_hbm(demand, kkt_inverse[0], boundary_bus[0], tie_count.reshape(1, region_count), part_bus.T, part_share.T))
    outer = swapped(outer, "region", 1)
    inner = swapped(inner, "region", 0)
    stacked, edge, params = pl.pallas_call(
        edge_kernel,
        out_shape=(jax.ShapeDtypeStruct((hours + 2 * slots, buses), BF16), row, table),
        in_specs=[VMEM] * 8,
        out_specs=(VMEM,) * 3,
        compiler_params=PARAMS,
        cost_estimate=pl.CostEstimate(flops=2 * hours * buses * buses, bytes_accessed=4 << 20, transcendentals=0),
        name="edge",
    )(demand, pick, matrix, *rows)
    edge = from_behind(edge, "hour")
    base, slot_matrix, dual, low, high, weight = pl.pallas_call(
        middle_kernel,
        out_shape=(
            wide,
            jax.ShapeDtypeStruct((2 * slots, buses), BF16),
            wide,
            wide,
            wide,
            jax.ShapeDtypeStruct((buses, parts - EARLY * LANES), BF16),
        ),
        in_specs=[VMEM] * 6,
        out_specs=(VMEM,) * 6,
        compiler_params=PARAMS,
        cost_estimate=pl.CostEstimate(flops=2 * 384 * buses * buses, bytes_accessed=12 << 20, transcendentals=0),
        name="middle",
    )(stacked, demand, params, matrix, part_bus, part_share)
    own_hours = hours // region_count
    price_shape = jax.ShapeDtypeStruct((hours, parts), BF16)
    direct = own_hours % 16 == 0 and region_count == 8
    price_buffer = [pltpu.VMEM((hours, parts), BF16)] if direct else []
    piece = jax.ShapeDtypeStruct((own_hours, parts), BF16)
    price_out = [price_shape]
    if direct:
        price_out = [piece] * (1 + len(SECOND)) + [
            jax.ShapeDtypeStruct((own_hours * (1 + len(relays)), parts), BF16) for relays in FIRST.values()
        ]
    angles, *price = pl.pallas_call(
        last_kernel,
        out_shape=(wide, *price_out),
        in_specs=[VMEM] * 11,
        out_specs=(VMEM,) * (1 + len(price_out)),
        scratch_shapes=price_buffer,
        compiler_params=PARAMS,
        name="second_angles",
    )(base, slot_matrix, outer, inner, edge, dual, low, high, early, weight, params)
    if direct:
        own, *price = price
        kept = dict(zip(SECOND, price))
        got = {step: crossed(v, step) for step, v in zip(FIRST, price[len(SECOND) :])}
        sums = []
        for step, sources in SECOND.items():
            places = [1 + FIRST[source].index(step) for source in sources]
            total = pl.pallas_call(
                functools.partial(relay_kernel, places),
                out_shape=piece,
                in_specs=[VMEM] * (1 + len(sources)),
                out_specs=VMEM,
                compiler_params=PARAMS,
                name="relay",
            )(kept[step], *(got[source] for source in sources))
            sums.append(crossed(total, step))
        pieces = [own] + list(got.values()) + sums
        after = total
    else:
        pieces = lax.all_to_all(price[0].reshape(region_count, own_hours, parts), "region", 0, 0, tiled=True)
        pieces = [pieces[i] for i in range(region_count)]
        after = pieces[0]
    angles = pl.pallas_call(
        store_kernel,
        out_shape=wide,
        in_specs=[VMEM, VMEM],
        out_specs=HBM,
        scratch_shapes=[pltpu.SemaphoreType.DMA],
        compiler_params=PARAMS,
        cost_estimate=pl.CostEstimate(flops=0, bytes_accessed=8 * hours * buses, transcendentals=0),
        name="store",
    )(angles, after)
    payment = pl.pallas_call(
        pay_kernel,
        out_shape=jax.ShapeDtypeStruct(cleared_mw.shape[1:], F32),
        in_specs=[VMEM] * (1 + len(pieces)),
        out_specs=VMEM,
        compiler_params=PARAMS,
        name="payment",
    )(cleared_mw[0], *pieces)
    return angles, payment[None]


def solution(mesh):
    return jax.shard_map(
        shards,
        mesh=mesh,
        in_specs=(
            P("region", None, None),
            P("hour", "region"),
            P("region"),
            P("region"),
            P("region"),
            P("region"),
            P("region"),
            P("region", None, None),
            P(),
            P(),
            P(),
            P("hour", "region", None),
        ),
        out_specs=(P("hour", "region"), P("hour", "region", None)),
        check_vma=False,
    )
```

```python
import functools

import jax
import jax.numpy as jnp
from jax import lax
from jax.experimental import pallas as pl
from jax.experimental.pallas import tpu as pltpu
from jax.sharding import PartitionSpec as P

BF16 = jnp.bfloat16
F32 = jnp.float32
I32 = jnp.int32
VMEM = pl.BlockSpec(memory_space=pltpu.VMEM)
HBM = pl.BlockSpec(memory_space=pltpu.HBM)
NT = (((1,), (1,)), ((), ()))
TN = (((0,), (0,)), ((), ()))
FIRST = {7: (), 2: (4,), 1: (4,), 3: ()}
SECOND = {4: (2, 1)}
LANES = 128
EARLY = 2
PARAMS = pltpu.CompilerParams(vmem_limit_bytes=16 * 1024 * 1024)


def in_hbm(*arrays):
    return [pltpu.with_memory_space_constraint(v, pltpu.HBM) for v in arrays]


def swapped(value, axis, parity):
    count = lax.axis_size(axis)
    pairs = []
    for low in range(parity, count, 2):
        high = (low + 1) % count
        pairs += [(low, high), (high, low)]
    return lax.ppermute(value, axis, pairs)


def crossed(value, step):
    return lax.ppermute(value, "region", [(i, i ^ step) for i in range(lax.axis_size("region"))])


def from_behind(value, axis):
    count = lax.axis_size(axis)
    return lax.ppermute(value, axis, [(i, (i + 1) % count) for i in range(count)])


def shares_by_bus(part_ref, share_ref, weight_ref, region, begin, end):
    buses = weight_ref.shape[0]
    taps = part_ref.shape[0]
    local = part_ref[...] - region * buses
    inside = jnp.logical_and(local >= 0, local < buses)
    local = jnp.where(inside, local, -1)
    upper = lax.shift_right_arithmetic(local, 7)
    lower = jnp.where(inside, jnp.bitwise_and(local, LANES - 1), -1)
    share = share_ref[...]
    half = LANES // 2
    for group in range(begin, end):
        lanes = slice(group * LANES, (group + 1) * LANES)
        out_lanes = slice((group - begin) * LANES, (group - begin + 1) * LANES)
        for part in range(2):
            ids = lax.broadcasted_iota(I32, (half, LANES), 0) + part * half
            values = [
                jnp.where(ids == lower[k : k + 1, lanes], share[k : k + 1, lanes], 0.0).astype(BF16) for k in range(taps)
            ]
            for a in range(buses // LANES):
                total = None
                for k in range(taps):
                    mask = jnp.where(upper[k : k + 1, lanes] == a, 1.0, 0.0)
                    mask = jnp.broadcast_to(mask, (half, LANES)).astype(BF16)
                    term = values[k] * mask
                    total = term if total is None else total + term
                weight_ref[a * LANES + part * half : a * LANES + (part + 1) * half, out_lanes] = total


def ends_kernel(
    demand_in, matrix_in, bus_in, count_in, part_in, share_in,
    inner_ref, outer_ref, matrix_ref, demand_ref, pick_ref, part_ref, share_ref, weight_ref,
    bus_ref, count_ref, sems,
):
    buses = matrix_ref.shape[0]
    copies = [
        pltpu.make_async_copy(source, target, sems.at[i])
        for i, (source, target) in enumerate(
            [
                (bus_in, bus_ref), (count_in, count_ref), (part_in, part_ref), (share_in, share_ref),
                (demand_in, demand_ref), (matrix_in, matrix_ref),
            ]
        )
    ]
    for copy in copies:
        copy.start()
    for copy in copies[:4]:
        copy.wait()

    region = lax.axis_index("region")
    region_count = count_ref.shape[1]
    odd = lax.rem(region, 2)
    slots = bus_ref.shape[1]
    left_region = lax.rem(region + region_count - 1, region_count)
    regions = lax.broadcasted_iota(I32, count_ref.shape, 1)
    counts = count_ref[...]
    left_count = jnp.sum(jnp.where(regions == left_region, counts, 0), axis=1, keepdims=True)
    right_count = jnp.sum(jnp.where(regions == region, counts, 0), axis=1, keepdims=True)
    ids = lax.broadcasted_iota(I32, (1, slots), 1)
    left_bus = jnp.where(ids < left_count, bus_ref[0:1, :], -1)
    right_bus = jnp.where(ids < right_count, bus_ref[1:2, :], -1)
    inner_bus = jnp.where(odd == 0, right_bus, left_bus)
    outer_bus = jnp.where(odd == 0, left_bus, right_bus)
    columns = jnp.transpose(jnp.concatenate([inner_bus, outer_bus] * 4, axis=0))
    lane = lax.broadcasted_iota(I32, (slots, buses), 1)
    for side in range(2):
        pick = (lane == columns[:, side : side + 1]).astype(F32).astype(BF16)
        pick_ref[side * slots : (side + 1) * slots, :] = pick
    shares_by_bus(part_ref, share_ref, weight_ref, region, 0, EARLY)
    copies[4].wait()
    right_side = jnp.transpose(demand_ref[...]).astype(BF16)
    copies[5].wait()
    slot_rows = jnp.dot(pick_ref[...], matrix_ref[...], preferred_element_type=F32).astype(BF16)
    ends = jnp.dot(slot_rows, right_side, preferred_element_type=F32).astype(BF16)
    inner_ref[...] = ends[:slots]
    outer_ref[...] = ends[slots:]


def edge_kernel(
    demand_ref, pick_ref, matrix_ref, quad_ref, lin_ref, cap_ref, ramp_ref, start_ref,
    stacked_ref, edge_ref, params_ref,
):
    hours, buses = demand_ref.shape
    stacked_ref[:hours, :] = demand_ref[...].astype(BF16)
    stacked_ref[hours:, :] = pick_ref[...]
    tail = demand_ref[pl.ds(hours - 16, 16), :].astype(BF16)
    angles = lax.dot_general(tail, matrix_ref[...], NT, preferred_element_type=F32)[15:]
    inverse, lin, cap, ramp = 1.0 / (quad_ref[...] + 1.0), lin_ref[...], cap_ref[...], ramp_ref[...]
    pad = jnp.zeros((3, buses), F32)
    params_ref[...] = jnp.concatenate([inverse, lin, cap, ramp, start_ref[...], pad], axis=0)
    target = (angles - lin) * inverse
    limited = jnp.minimum(jnp.maximum(target, -ramp), ramp)
    edge_ref[...] = jnp.minimum(jnp.maximum(limited, 0.0), cap)


def middle_kernel(
    stacked_ref, demand_ref, params_ref, matrix_ref, part_ref, share_ref,
    base_ref, slot_matrix_ref, dual_ref, low_ref, high_ref, weight_ref,
):
    hours, buses = demand_ref.shape
    region = lax.axis_index("region")
    block = lax.axis_index("hour")
    inverse, lin, cap, ramp, start = (params_ref[i : i + 1, :] for i in range(5))
    demand = demand_ref[...]
    turned = jnp.transpose(matrix_ref[...])
    product = jnp.dot(stacked_ref[...], turned, preferred_element_type=F32)
    slot_matrix_ref[...] = product[hours:].astype(BF16)
    angles = product[:hours]
    row = lax.broadcasted_iota(I32, (hours, buses), 0)
    first = jnp.logical_and(row == 0, block == 0)
    prior = jnp.where(first, jnp.broadcast_to(start, (hours, buses)), 0.0)
    target = (angles - lin) * inverse
    limited = jnp.minimum(jnp.maximum(target, prior - ramp), prior + ramp)
    generation = jnp.minimum(jnp.maximum(limited, 0.0), cap)
    dual = angles - generation
    dual_ref[...] = dual
    right_side = (demand + (generation - dual)).astype(BF16)
    before = pltpu.roll(generation, 1, 0)
    low_ref[...] = jnp.minimum(jnp.maximum(before - ramp, 0.0), cap)
    high_ref[...] = jnp.minimum(jnp.maximum(before + ramp, 0.0), cap)
    base_ref[...] = jnp.dot(right_side, turned, preferred_element_type=F32)
    shares_by_bus(part_ref, share_ref, weight_ref, region, EARLY, part_ref.shape[1] // LANES)


def last_kernel(
    base_ref, slot_matrix_ref, outer_ref, inner_ref, edge_ref, dual_ref, low_ref, high_ref, early_ref, weight_ref, params_ref,
    angles_ref, *rest,
):
    *piece_refs, price_ref = rest
    hours, buses = base_ref.shape
    block = lax.axis_index("hour")
    inverse, lin, cap, ramp, start = (params_ref[i : i + 1, :] for i in range(5))
    far = jnp.concatenate([inner_ref[...], outer_ref[...]], axis=0)
    angles = base_ref[...] + lax.dot_general(far, slot_matrix_ref[...], TN, preferred_element_type=F32)
    angles_ref[...] = angles
    prior = jnp.where(block == 0, start, edge_ref[...])
    low_first = jnp.minimum(jnp.maximum(prior - ramp, 0.0), cap)
    high_first = jnp.minimum(jnp.maximum(prior + ramp, 0.0), cap)
    top = 16
    first = lax.broadcasted_iota(I32, (top, buses), 0) == 0
    total = angles + dual_ref[...]
    target = (total - lin) * inverse
    low = jnp.where(first, low_first, low_ref[:top, :])
    high = jnp.where(first, high_first, high_ref[:top, :])
    head = jnp.minimum(jnp.maximum(target[:top], low), high)
    rest = jnp.minimum(jnp.maximum(target[top:], low_ref[top:, :]), high_ref[top:, :])
    lmp = (total - jnp.concatenate([head, rest], axis=0)).astype(BF16)
    cut = early_ref.shape[1]
    price_ref[:, :cut] = jnp.dot(lmp, early_ref[...], preferred_element_type=F32).astype(BF16)
    price_ref[:, cut:] = jnp.dot(lmp, weight_ref[...], preferred_element_type=F32).astype(BF16)
    region = lax.axis_index("region")
    if piece_refs:
        rows = piece_refs[0].shape[0]

        def piece(step):
            owner = jnp.bitwise_xor(region, step)
            return price_ref[pl.ds(pl.multiple_of(owner * rows, rows), rows), :]

        kept = [0] + list(SECOND)
        for step, kept_ref in zip(kept, piece_refs):
            kept_ref[...] = piece(step)
        for (step, relays), sent_ref in zip(FIRST.items(), piece_refs[len(kept) :]):
            for i, k in enumerate([step] + [step ^ relay for relay in relays]):
                sent_ref[i * rows : (i + 1) * rows, :] = piece(k)


def relay_kernel(places, kept_ref, *refs):
    *got_refs, sum_ref = refs
    rows = kept_ref.shape[0]
    total = kept_ref[...].astype(F32)
    for place, got_ref in zip(places, got_refs):
        total = total + got_ref[place * rows : (place + 1) * rows, :].astype(F32)
    sum_ref[...] = total.astype(BF16)


def store_kernel(angles_ref, after_ref, angles_out, sem):
    copy = pltpu.make_async_copy(angles_ref, angles_out, sem)
    copy.start()
    copy.wait()


def pay_kernel(cleared_ref, *refs):
    *piece_refs, out_ref = refs
    rows = out_ref.shape[0]
    total = piece_refs[0][:rows, :].astype(F32)
    for piece_ref in piece_refs[1:]:
        total = total + piece_ref[:rows, :].astype(F32)
    out_ref[...] = cleared_ref[...] * total


def shards(
    kkt_inverse, demand, cost_quad, cost_lin, capacity, ramp, gen_start, boundary_bus, tie_count,
    part_bus, part_share, cleared_mw,
):
    region_count = lax.axis_size("region")
    hours, buses = demand.shape
    slots = boundary_bus.shape[2]
    parts, taps = part_bus.shape
    rows = [v.reshape(1, buses) for v in (cost_quad, cost_lin, capacity, ramp, gen_start)]
    wide = jax.ShapeDtypeStruct((hours, buses), F32)
    row = jax.ShapeDtypeStruct((1, buses), F32)
    square = jax.ShapeDtypeStruct((buses, buses), BF16)
    ends = jax.ShapeDtypeStruct((slots, hours), BF16)
    table = jax.ShapeDtypeStruct((8, buses), F32)
    inner, outer, matrix, demand, pick, part_bus, part_share, early = pl.pallas_call(
        ends_kernel,
        out_shape=(
            ends, ends, square, wide,
            jax.ShapeDtypeStruct((2 * slots, buses), BF16),
            jax.ShapeDtypeStruct((taps, parts), I32),
            jax.ShapeDtypeStruct((taps, parts), F32),
            jax.ShapeDtypeStruct((buses, EARLY * LANES), BF16),
        ),
        in_specs=[HBM] * 6,
        out_specs=(VMEM,) * 8,
        scratch_shapes=[
            pltpu.VMEM((2, slots), I32),
            pltpu.VMEM((1, region_count), I32),
            pltpu.SemaphoreType.DMA((6,)),
        ],
        compiler_params=PARAMS,
        name="ends",
    )(*in_hbm(demand, kkt_inverse[0], boundary_bus[0], tie_count.reshape(1, region_count), part_bus.T, part_share.T))
    outer = swapped(outer, "region", 1)
    inner = swapped(inner, "region", 0)
    stacked, edge, params = pl.pallas_call(
        edge_kernel,
        out_shape=(jax.ShapeDtypeStruct((hours + 2 * slots, buses), BF16), row, table),
        in_specs=[VMEM] * 8,
        out_specs=(VMEM,) * 3,
        compiler_params=PARAMS,
        cost_estimate=pl.CostEstimate(flops=2 * hours * buses * buses, bytes_accessed=4 << 20, transcendentals=0),
        name="edge",
    )(demand, pick, matrix, *rows)
    edge = from_behind(edge, "hour")
    base, slot_matrix, dual, low, high, weight = pl.pallas_call(
        middle_kernel,
        out_shape=(
            wide,
            jax.ShapeDtypeStruct((2 * slots, buses), BF16),
            wide,
            wide,
            wide,
            jax.ShapeDtypeStruct((buses, parts - EARLY * LANES), BF16),
        ),
        in_specs=[VMEM] * 6,
        out_specs=(VMEM,) * 6,
        compiler_params=PARAMS,
        cost_estimate=pl.CostEstimate(flops=2 * 384 * buses * buses, bytes_accessed=12 << 20, transcendentals=0),
        name="middle",
    )(stacked, demand, params, matrix, part_bus, part_share)
    own_hours = hours // region_count
    price_shape = jax.ShapeDtypeStruct((hours, parts), BF16)
    direct = own_hours % 16 == 0 and region_count == 8
    price_buffer = [pltpu.VMEM((hours, parts), BF16)] if direct else []
    piece = jax.ShapeDtypeStruct((own_hours, parts), BF16)
    price_out = [price_shape]
    if direct:
        price_out = [piece] * (1 + len(SECOND)) + [
            jax.ShapeDtypeStruct((own_hours * (1 + len(relays)), parts), BF16) for relays in FIRST.values()
        ]
    angles, *price = pl.pallas_call(
        last_kernel,
        out_shape=(wide, *price_out),
        in_specs=[VMEM] * 11,
        out_specs=(VMEM,) * (1 + len(price_out)),
        scratch_shapes=price_buffer,
        compiler_params=PARAMS,
        name="second_angles",
    )(base, slot_matrix, outer, inner, edge, dual, low, high, early, weight, params)
    if direct:
        own, *price = price
        kept = dict(zip(SECOND, price))
        got = {step: crossed(v, step) for step, v in zip(FIRST, price[len(SECOND) :])}
        sums = []
        for step, sources in SECOND.items():
            places = [1 + FIRST[source].index(step) for source in sources]
            total = pl.pallas_call(
                functools.partial(relay_kernel, places),
                out_shape=piece,
                in_specs=[VMEM] * (1 + len(sources)),
                out_specs=VMEM,
                compiler_params=PARAMS,
                name="relay",
            )(kept[step], *(got[source] for source in sources))
            sums.append(crossed(total, step))
        pieces = [own] + list(got.values()) + sums
        after = total
    else:
        pieces = lax.all_to_all(price[0].reshape(region_count, own_hours, parts), "region", 0, 0, tiled=True)
        pieces = [pieces[i] for i in range(region_count)]
        after = pieces[0]
    angles = pl.pallas_call(
        store_kernel,
        out_shape=wide,
        in_specs=[VMEM, VMEM],
        out_specs=HBM,
        scratch_shapes=[pltpu.SemaphoreType.DMA],
        compiler_params=PARAMS,
        cost_estimate=pl.CostEstimate(flops=0, bytes_accessed=8 * hours * buses, transcendentals=0),
        name="store",
    )(angles, after)
    payment = pl.pallas_call(
        pay_kernel,
        out_shape=jax.ShapeDtypeStruct(cleared_mw.shape[1:], F32),
        in_specs=[VMEM] * (1 + len(pieces)),
        out_specs=VMEM,
        compiler_params=PARAMS,
        name="payment",
    )(cleared_mw[0], *pieces)
    return angles, payment[None]


def solution(mesh):
    return jax.shard_map(
        shards,
        mesh=mesh,
        in_specs=(
            P("region", None, None),
            P("hour", "region"),
            P("region"),
            P("region"),
            P("region"),
            P("region"),
            P("region"),
            P("region", None, None),
            P(),
            P(),
            P(),
            P("hour", "region", None),
        ),
        out_specs=(P("hour", "region"), P("hour", "region", None)),
        check_vma=False,
    )
```

```python
import functools

import jax
import jax.numpy as jnp
from jax import lax
from jax.experimental import pallas as pl
from jax.experimental.pallas import tpu as pltpu
from jax.sharding import PartitionSpec as P

BF16 = jnp.bfloat16
F32 = jnp.float32
I32 = jnp.int32
VMEM = pl.BlockSpec(memory_space=pltpu.VMEM)
HBM = pl.BlockSpec(memory_space=pltpu.HBM)
NT = (((1,), (1,)), ((), ()))
TN = (((0,), (0,)), ((), ()))
FIRST = {7: (), 2: (4,), 1: (4,), 3: ()}
SECOND = {4: (2, 1)}
LANES = 128
EARLY = 2
PARAMS = pltpu.CompilerParams(vmem_limit_bytes=16 * 1024 * 1024)


def in_hbm(*arrays):
    return [pltpu.with_memory_space_constraint(v, pltpu.HBM) for v in arrays]


def swapped(value, axis, parity):
    count = lax.axis_size(axis)
    pairs = []
    for low in range(parity, count, 2):
        high = (low + 1) % count
        pairs += [(low, high), (high, low)]
    return lax.ppermute(value, axis, pairs)


def crossed(value, step):
    return lax.ppermute(value, "region", [(i, i ^ step) for i in range(lax.axis_size("region"))])


def from_behind(value, axis):
    count = lax.axis_size(axis)
    return lax.ppermute(value, axis, [(i, (i + 1) % count) for i in range(count)])


def shares_by_bus(part_ref, share_ref, weight_ref, region, begin, end):
    buses = weight_ref.shape[0]
    taps = part_ref.shape[0]
    local = part_ref[...] - region * buses
    inside = jnp.logical_and(local >= 0, local < buses)
    local = jnp.where(inside, local, -1)
    upper = lax.shift_right_arithmetic(local, 7)
    lower = jnp.where(inside, jnp.bitwise_and(local, LANES - 1), -1)
    share = share_ref[...]
    half = LANES // 2
    for group in range(begin, end):
        lanes = slice(group * LANES, (group + 1) * LANES)
        out_lanes = slice((group - begin) * LANES, (group - begin + 1) * LANES)
        for part in range(2):
            ids = lax.broadcasted_iota(I32, (half, LANES), 0) + part * half
            values = [
                jnp.where(ids == lower[k : k + 1, lanes], share[k : k + 1, lanes], 0.0).astype(BF16) for k in range(taps)
            ]
            for a in range(buses // LANES):
                total = None
                for k in range(taps):
                    mask = jnp.where(upper[k : k + 1, lanes] == a, 1.0, 0.0)
                    mask = jnp.broadcast_to(mask, (half, LANES)).astype(BF16)
                    term = values[k] * mask
                    total = term if total is None else total + term
                weight_ref[a * LANES + part * half : a * LANES + (part + 1) * half, out_lanes] = total


def ends_kernel(
    demand_in, matrix_in, bus_in, count_in, part_in, share_in,
    inner_ref, outer_ref, matrix_ref, demand_ref, pick_ref, part_ref, share_ref, weight_ref,
    bus_ref, count_ref, sems,
):
    buses = matrix_ref.shape[0]
    copies = [
        pltpu.make_async_copy(source, target, sems.at[i])
        for i, (source, target) in enumerate(
            [
                (bus_in, bus_ref), (count_in, count_ref), (part_in, part_ref), (share_in, share_ref),
                (demand_in, demand_ref), (matrix_in, matrix_ref),
            ]
        )
    ]
    for copy in copies:
        copy.start()
    for copy in copies[:4]:
        copy.wait()

    region = lax.axis_index("region")
    region_count = count_ref.shape[1]
    odd = lax.rem(region, 2)
    slots = bus_ref.shape[1]
    left_region = lax.rem(region + region_count - 1, region_count)
    regions = lax.broadcasted_iota(I32, count_ref.shape, 1)
    counts = count_ref[...]
    left_count = jnp.sum(jnp.where(regions == left_region, counts, 0), axis=1, keepdims=True)
    right_count = jnp.sum(jnp.where(regions == region, counts, 0), axis=1, keepdims=True)
    ids = lax.broadcasted_iota(I32, (1, slots), 1)
    left_bus = jnp.where(ids < left_count, bus_ref[0:1, :], -1)
    right_bus = jnp.where(ids < right_count, bus_ref[1:2, :], -1)
    inner_bus = jnp.where(odd == 0, right_bus, left_bus)
    outer_bus = jnp.where(odd == 0, left_bus, right_bus)
    columns = jnp.transpose(jnp.concatenate([inner_bus, outer_bus] * 4, axis=0))
    lane = lax.broadcasted_iota(I32, (slots, buses), 1)
    for side in range(2):
        pick = (lane == columns[:, side : side + 1]).astype(F32).astype(BF16)
        pick_ref[side * slots : (side + 1) * slots, :] = pick
    shares_by_bus(part_ref, share_ref, weight_ref, region, 0, EARLY)
    copies[4].wait()
    right_side = jnp.transpose(demand_ref[...]).astype(BF16)
    copies[5].wait()
    slot_rows = jnp.dot(pick_ref[...], matrix_ref[...], preferred_element_type=F32).astype(BF16)
    ends = jnp.dot(slot_rows, right_side, preferred_element_type=F32).astype(BF16)
    inner_ref[...] = ends[:slots]
    outer_ref[...] = ends[slots:]


def edge_kernel(
    demand_ref, pick_ref, matrix_ref, quad_ref, lin_ref, cap_ref, ramp_ref, start_ref,
    stacked_ref, edge_ref, params_ref,
):
    hours, buses = demand_ref.shape
    stacked_ref[:hours, :] = demand_ref[...].astype(BF16)
    stacked_ref[hours:, :] = pick_ref[...]
    tail = demand_ref[pl.ds(hours - 16, 16), :].astype(BF16)
    angles = lax.dot_general(tail, matrix_ref[...], NT, preferred_element_type=F32)[15:]
    inverse, lin, cap, ramp = 1.0 / (quad_ref[...] + 1.0), lin_ref[...], cap_ref[...], ramp_ref[...]
    pad = jnp.zeros((3, buses), F32)
    params_ref[...] = jnp.concatenate([inverse, lin, cap, ramp, start_ref[...], pad], axis=0)
    target = (angles - lin) * inverse
    limited = jnp.minimum(jnp.maximum(target, -ramp), ramp)
    edge_ref[...] = jnp.minimum(jnp.maximum(limited, 0.0), cap)


def middle_kernel(
    stacked_ref, demand_ref, params_ref, matrix_ref, part_ref, share_ref,
    base_ref, slot_matrix_ref, dual_ref, low_ref, high_ref, weight_ref,
):
    hours, buses = demand_ref.shape
    region = lax.axis_index("region")
    block = lax.axis_index("hour")
    inverse, lin, cap, ramp, start = (params_ref[i : i + 1, :] for i in range(5))
    demand = demand_ref[...]
    turned = jnp.transpose(matrix_ref[...])
    product = jnp.dot(stacked_ref[...], turned, preferred_element_type=F32)
    slot_matrix_ref[...] = product[hours:].astype(BF16)
    angles = product[:hours]
    row = lax.broadcasted_iota(I32, (hours, buses), 0)
    first = jnp.logical_and(row == 0, block == 0)
    prior = jnp.where(first, jnp.broadcast_to(start, (hours, buses)), 0.0)
    target = (angles - lin) * inverse
    limited = jnp.minimum(jnp.maximum(target, prior - ramp), prior + ramp)
    generation = jnp.minimum(jnp.maximum(limited, 0.0), cap)
    dual = angles - generation
    dual_ref[...] = dual
    right_side = (demand + (generation - dual)).astype(BF16)
    before = pltpu.roll(generation, 1, 0)
    low_ref[...] = jnp.minimum(jnp.maximum(before - ramp, 0.0), cap)
    high_ref[...] = jnp.minimum(jnp.maximum(before + ramp, 0.0), cap)
    base_ref[...] = jnp.dot(right_side, turned, preferred_element_type=F32)
    shares_by_bus(part_ref, share_ref, weight_ref, region, EARLY, part_ref.shape[1] // LANES)


def last_kernel(
    base_ref, slot_matrix_ref, outer_ref, inner_ref, edge_ref, dual_ref, low_ref, high_ref, early_ref, weight_ref, params_ref,
    angles_ref, *rest,
):
    *piece_refs, price_ref = rest
    hours, buses = base_ref.shape
    block = lax.axis_index("hour")
    inverse, lin, cap, ramp, start = (params_ref[i : i + 1, :] for i in range(5))
    far = jnp.concatenate([inner_ref[...], outer_ref[...]], axis=0)
    angles = base_ref[...] + lax.dot_general(far, slot_matrix_ref[...], TN, preferred_element_type=F32)
    angles_ref[...] = angles
    prior = jnp.where(block == 0, start, edge_ref[...])
    low_first = jnp.minimum(jnp.maximum(prior - ramp, 0.0), cap)
    high_first = jnp.minimum(jnp.maximum(prior + ramp, 0.0), cap)
    top = 16
    first = lax.broadcasted_iota(I32, (top, buses), 0) == 0
    total = angles + dual_ref[...]
    target = (total - lin) * inverse
    low = jnp.where(first, low_first, low_ref[:top, :])
    high = jnp.where(first, high_first, high_ref[:top, :])
    head = jnp.minimum(jnp.maximum(target[:top], low), high)
    rest = jnp.minimum(jnp.maximum(target[top:], low_ref[top:, :]), high_ref[top:, :])
    lmp = (total - jnp.concatenate([head, rest], axis=0)).astype(BF16)
    cut = early_ref.shape[1]
    price_ref[:, :cut] = jnp.dot(lmp, early_ref[...], preferred_element_type=F32).astype(BF16)
    price_ref[:, cut:] = jnp.dot(lmp, weight_ref[...], preferred_element_type=F32).astype(BF16)
    region = lax.axis_index("region")
    if piece_refs:
        rows = piece_refs[0].shape[0]

        def piece(step):
            owner = jnp.bitwise_xor(region, step)
            return price_ref[pl.ds(pl.multiple_of(owner * rows, rows), rows), :]

        kept = [0] + list(SECOND)
        for step, kept_ref in zip(kept, piece_refs):
            kept_ref[...] = piece(step)
        for (step, relays), sent_ref in zip(FIRST.items(), piece_refs[len(kept) :]):
            for i, k in enumerate([step] + [step ^ relay for relay in relays]):
                sent_ref[i * rows : (i + 1) * rows, :] = piece(k)


def relay_kernel(places, kept_ref, *refs):
    *got_refs, sum_ref = refs
    rows = kept_ref.shape[0]
    total = kept_ref[...].astype(F32)
    for place, got_ref in zip(places, got_refs):
        total = total + got_ref[place * rows : (place + 1) * rows, :].astype(F32)
    sum_ref[...] = total.astype(BF16)


def store_kernel(angles_ref, after_ref, angles_out, sem):
    copy = pltpu.make_async_copy(angles_ref, angles_out, sem)
    copy.start()
    copy.wait()


def shards(
    kkt_inverse, demand, cost_quad, cost_lin, capacity, ramp, gen_start, boundary_bus, tie_count,
    part_bus, part_share, cleared_mw,
):
    region_count = lax.axis_size("region")
    hours, buses = demand.shape
    slots = boundary_bus.shape[2]
    parts, taps = part_bus.shape
    rows = [v.reshape(1, buses) for v in (cost_quad, cost_lin, capacity, ramp, gen_start)]
    wide = jax.ShapeDtypeStruct((hours, buses), F32)
    row = jax.ShapeDtypeStruct((1, buses), F32)
    square = jax.ShapeDtypeStruct((buses, buses), BF16)
    ends = jax.ShapeDtypeStruct((slots, hours), BF16)
    table = jax.ShapeDtypeStruct((8, buses), F32)
    inner, outer, matrix, demand, pick, part_bus, part_share, early = pl.pallas_call(
        ends_kernel,
        out_shape=(
            ends, ends, square, wide,
            jax.ShapeDtypeStruct((2 * slots, buses), BF16),
            jax.ShapeDtypeStruct((taps, parts), I32),
            jax.ShapeDtypeStruct((taps, parts), F32),
            jax.ShapeDtypeStruct((buses, EARLY * LANES), BF16),
        ),
        in_specs=[HBM] * 6,
        out_specs=(VMEM,) * 8,
        scratch_shapes=[
            pltpu.VMEM((2, slots), I32),
            pltpu.VMEM((1, region_count), I32),
            pltpu.SemaphoreType.DMA((6,)),
        ],
        compiler_params=PARAMS,
        name="ends",
    )(*in_hbm(demand, kkt_inverse[0], boundary_bus[0], tie_count.reshape(1, region_count), part_bus.T, part_share.T))
    outer = swapped(outer, "region", 1)
    inner = swapped(inner, "region", 0)
    stacked, edge, params = pl.pallas_call(
        edge_kernel,
        out_shape=(jax.ShapeDtypeStruct((hours + 2 * slots, buses), BF16), row, table),
        in_specs=[VMEM] * 8,
        out_specs=(VMEM,) * 3,
        compiler_params=PARAMS,
        cost_estimate=pl.CostEstimate(flops=2 * hours * buses * buses, bytes_accessed=4 << 20, transcendentals=0),
        name="edge",
    )(demand, pick, matrix, *rows)
    edge = from_behind(edge, "hour")
    base, slot_matrix, dual, low, high, weight = pl.pallas_call(
        middle_kernel,
        out_shape=(
            wide,
            jax.ShapeDtypeStruct((2 * slots, buses), BF16),
            wide,
            wide,
            wide,
            jax.ShapeDtypeStruct((buses, parts - EARLY * LANES), BF16),
        ),
        in_specs=[VMEM] * 6,
        out_specs=(VMEM,) * 6,
        compiler_params=PARAMS,
        cost_estimate=pl.CostEstimate(flops=2 * 384 * buses * buses, bytes_accessed=12 << 20, transcendentals=0),
        name="middle",
    )(stacked, demand, params, matrix, part_bus, part_share)
    own_hours = hours // region_count
    price_shape = jax.ShapeDtypeStruct((hours, parts), BF16)
    direct = own_hours % 16 == 0 and region_count == 8
    price_buffer = [pltpu.VMEM((hours, parts), BF16)] if direct else []
    piece = jax.ShapeDtypeStruct((own_hours, parts), BF16)
    price_out = [price_shape]
    if direct:
        price_out = [piece] * (1 + len(SECOND)) + [
            jax.ShapeDtypeStruct((own_hours * (1 + len(relays)), parts), BF16) for relays in FIRST.values()
        ]
    angles, *price = pl.pallas_call(
        last_kernel,
        out_shape=(wide, *price_out),
        in_specs=[VMEM] * 11,
        out_specs=(VMEM,) * (1 + len(price_out)),
        scratch_shapes=price_buffer,
        compiler_params=PARAMS,
        name="second_angles",
    )(base, slot_matrix, outer, inner, edge, dual, low, high, early, weight, params)
    if direct:
        own, *price = price
        kept = dict(zip(SECOND, price))
        got = {step: crossed(v, step) for step, v in zip(FIRST, price[len(SECOND) :])}
        sums = []
        for step, sources in SECOND.items():
            places = [1 + FIRST[source].index(step) for source in sources]
            total = pl.pallas_call(
                functools.partial(relay_kernel, places),
                out_shape=piece,
                in_specs=[VMEM] * (1 + len(sources)),
                out_specs=VMEM,
                compiler_params=PARAMS,
                name="relay",
            )(kept[step], *(got[source] for source in sources))
            sums.append(crossed(total, step))
        pieces = [own] + list(got.values()) + sums
        after = total
    else:
        pieces = lax.all_to_all(price[0].reshape(region_count, own_hours, parts), "region", 0, 0, tiled=True)
        pieces = [pieces[i] for i in range(region_count)]
        after = pieces[0]
    angles = pl.pallas_call(
        store_kernel,
        out_shape=wide,
        in_specs=[VMEM, VMEM],
        out_specs=HBM,
        scratch_shapes=[pltpu.SemaphoreType.DMA],
        compiler_params=PARAMS,
        cost_estimate=pl.CostEstimate(flops=0, bytes_accessed=8 * hours * buses, transcendentals=0),
        name="store",
    )(angles, after)
    total = pieces[0][:own_hours].astype(F32)
    for piece in pieces[1:]:
        total = total + piece[:own_hours].astype(F32)
    payment = cleared_mw[0] * total
    return angles, payment[None]


def solution(mesh):
    return jax.shard_map(
        shards,
        mesh=mesh,
        in_specs=(
            P("region", None, None),
            P("hour", "region"),
            P("region"),
            P("region"),
            P("region"),
            P("region"),
            P("region"),
            P("region", None, None),
            P(),
            P(),
            P(),
            P("hour", "region", None),
        ),
        out_specs=(P("hour", "region"), P("hour", "region", None)),
        check_vma=False,
    )
```
